512 devices in a mesh: slab: 128 (over y, z, core), sub: 4 (over x).
Axes of the slice: x: 4, y: 4, z: 16, core: 2. Of those that a mesh axis runs over, the one named last changes fastest.
Arguments:
- adjoint: float32 [80, 262144], P(None, ('slab', 'sub')), may hold values from -6 to 6
- elem_scale: float32 [262144], P(('slab', 'sub')), may hold values from 0.5 to 2
- cluster: int32 [262144], P(('slab', 'sub')), may hold values from 0 to 2
- face_links: int32 [4, 262144], P(None, ('slab', 'sub')), may hold values from 0 to 1023
- halo_list: int32 [2, 131072], P(None, ('slab', 'sub')), may hold values from 0 to 511, as said below
- k_matrix: float32 [80, 80], replicated, may hold values from -0.625 to 0.625
- w_self: float32 [80, 80], replicated, may hold values from -0.625 to 0.625
- w_neighbour: float32 [80, 320], replicated, may hold values from -0.3125 to 0.3125
Outputs:
- result: float32 [80, 262144], P(None, ('slab', 'sub'))
The draws below stay inside these ranges and needn't reach their ends.
Inputs may be any that keep to these rules, and one draw needn't show every extreme that they name: `face_links`: on each device, a value below 512 names its own element; 512 + k names slot k of the received halo columns in the order of the steps. `halo_list`: on each device the 512 listed elements are distinct; each of the four sides of 128 listed elements holds at most 48 elements of any one cluster, and exactly 48 of two clusters.
All inputs are finite; a program needn't handle non-finite values.
Results may differ from the reference program's by a relative error of at most 0.0001.
Values sent between devices are 32-bit elements; how exact they have to be, the bound alone decides.
A program may use at most 64 MiB of HBM per device.

```python
import math
import jax
import jax.numpy as jnp
from jax import lax

Q = 80
E_DEV = 512
HALO = 128
CAP = 48
ELEMS = 262144
N_SLAB = 128
N_SUB = 4


def device_layout(dev_key):
    keys = jax.random.split(dev_key, 4)
    order = jax.random.permutation(keys[0], E_DEV).astype(jnp.int32)
    slots = order[:4 * HALO]
    steps_row = jnp.arange(HALO, dtype=jnp.int32)
    base = (steps_row >= CAP).astype(jnp.int32) + (steps_row >= 2 * CAP).astype(jnp.int32)
    labels = jax.vmap(lambda k: jax.random.permutation(k, 3).astype(jnp.int32))(jax.random.split(keys[1], 4))
    side_clusters = jnp.take_along_axis(labels, jnp.broadcast_to(base[None, :], (4, HALO)), axis=1)
    shuffles = jax.vmap(lambda k: jax.random.permutation(k, HALO).astype(jnp.int32))(jax.random.split(keys[2], 4))
    side_clusters = jnp.take_along_axis(side_clusters, shuffles, axis=1)
    others = jax.random.randint(keys[3], (E_DEV,), 0, 3, dtype=jnp.int32)
    clusters = others.at[slots].set(side_clusters.reshape(-1))
    return (clusters, slots.reshape(2, 2 * HALO))


def whole_layout(key):
    dev_keys = jax.random.split(key, N_SLAB * N_SUB)
    clusters, lists = jax.vmap(device_layout)(dev_keys)
    return (clusters.reshape(-1), jnp.transpose(lists, (1, 0, 2)).reshape(2, -1))


def draw_cluster(key, part):
    return whole_layout(key)[0]


def draw_halo_list(key, part):
    return whole_layout(key)[1]


def set_ends(values, rng, least, top_value):
    longest = values.shape.index(max(values.shape))
    spots = []
    for shift in (0, 1):
        where = [jax.random.randint(jax.random.fold_in(rng, axis), (), 0, length) for axis, length in enumerate(values.shape)]
        where[longest] = (where[longest] + shift) % values.shape[longest]
        spots.append(tuple(where))
    return values.at[spots[0]].set(least).at[spots[1]].set(top_value)


def level_of(stream_key, dims, cuts, least, top_value):
    def one(axis_at, blocks):
        heights = jax.random.uniform(jax.random.fold_in(jax.random.fold_in(stream_key, 6), axis_at), (blocks,), jnp.float32, least / len(cuts), top_value / len(cuts))
        return jnp.repeat(jnp.exp(heights), dims[axis_at] // blocks).reshape((-1,) + (1,) * (len(dims) - axis_at - 1))

    loudness = one(*cuts[0])
    for cut in cuts[1:]:
        loudness = loudness * one(*cut)
    return loudness


def normal_values(rng, shape, deviation, most, pieces=(), held_as=jnp.bfloat16):
    result = jax.random.normal(rng, shape, jnp.float32) * deviation
    if len(pieces) > 0:
        result = level_of(rng, shape, pieces, -0.22, 0.18) * result
    return jnp.clip(result, min=-most, max=most).astype(held_as)


def setup_inputs(seed: int = 0) -> dict:
    key_list = jax.random.split(jax.random.key(seed), 9)
    return {
        "adjoint": normal_values(key_list[0], (Q, ELEMS), 1.0, 6.0, ((1, 512),), jnp.float32),
        "elem_scale": jnp.clip(jnp.exp(math.log(2.0) - 1.3862944 * jax.random.uniform(key_list[1], (ELEMS,), jnp.float32) ** level_of(key_list[1], (ELEMS,), ((0, 512),), -0.2, 0.2)), 0.5, 2.0),
        "cluster": draw_cluster(jax.random.fold_in(key_list[8], 71), 0),
        "face_links": set_ends(jax.random.randint(key_list[3], (4, ELEMS), 0, E_DEV + 4 * HALO), jax.random.fold_in(key_list[3], 1), 0, (E_DEV + 4 * HALO) - 1).astype(jnp.int32),
        "halo_list": draw_halo_list(jax.random.fold_in(key_list[8], 71), 0),
        "k_matrix": normal_values(key_list[5], (Q, Q), Q ** -0.5, 0.625, (), jnp.float32),
        "w_self": normal_values(key_list[6], (Q, Q), Q ** -0.5, 0.625, (), jnp.float32),
        "w_neighbour": normal_values(key_list[7], (Q, 4 * Q), (4 * Q) ** -0.5, 0.3125, (), jnp.float32),
    }


time_step = 0.125


def predict(source, scale_row, k_matrix, step_size):
    total = source
    current = source
    for degree in range(1, 4):
        current = (step_size / (degree + 1)) * scale_row * jnp.dot(k_matrix, current, precision=lax.Precision.HIGHEST)
        total = total + current
    return total


def neighbour_sum(predicted, face_links, halo_list, w_neighbour):
    blocks = predicted.reshape(Q, N_SLAB, N_SUB, E_DEV)
    halo_rows = halo_list.reshape(2, N_SLAB, N_SUB, 2 * HALO)
    slab_send = jnp.take_along_axis(blocks, jnp.broadcast_to(halo_rows[0][None], (Q, N_SLAB, N_SUB, 2 * HALO)), axis=3)
    sub_send = jnp.take_along_axis(blocks, jnp.broadcast_to(halo_rows[1][None], (Q, N_SLAB, N_SUB, 2 * HALO)), axis=3)
    zero_slab = jnp.zeros((Q, 1, N_SUB, HALO), jnp.float32)
    zero_sub = jnp.zeros((Q, N_SLAB, 1, HALO), jnp.float32)
    slab_left = jnp.concatenate([zero_slab, slab_send[:, :-1, :, HALO:]], axis=1)
    slab_right = jnp.concatenate([slab_send[:, 1:, :, :HALO], zero_slab], axis=1)
    sub_left = jnp.concatenate([zero_sub, sub_send[:, :, :-1, HALO:]], axis=2)
    sub_right = jnp.concatenate([sub_send[:, :, 1:, :HALO], zero_sub], axis=2)
    extended = jnp.concatenate([blocks, slab_left, slab_right, sub_left, sub_right], axis=3)
    links = face_links.reshape(4, N_SLAB, N_SUB, E_DEV)
    total = jnp.zeros((Q, ELEMS), jnp.float32)
    for face_id in range(4):
        picked = jnp.take_along_axis(extended, jnp.broadcast_to(links[face_id][None], (Q, N_SLAB, N_SUB, E_DEV)), axis=3)
        total = total + jnp.dot(w_neighbour[:, face_id * Q:(face_id + 1) * Q], picked.reshape(Q, ELEMS), precision=lax.Precision.HIGHEST)
    return total


def reference(adjoint, elem_scale, cluster, face_links, halo_list, k_matrix, w_self, w_neighbour):
    scale_row = elem_scale[None, :]
    for substep in (3, 2, 1, 0):
        for rate_level in (2, 1, 0):
            if (substep + 1) % (2 ** rate_level) == 0:
                step_size = time_step * (2.0 ** rate_level)
                active = (cluster == rate_level).astype(jnp.float32)[None, :]
                predicted = predict(adjoint * active, scale_row, k_matrix, step_size)
                coupled = neighbour_sum(predicted, face_links, halo_list, w_neighbour)
                change = scale_row * (jnp.dot(w_self, predicted, precision=lax.Precision.HIGHEST) + coupled)
                adjoint = adjoint + step_size * change
    return adjoint
```

```python
import functools

import jax
import jax.numpy as jnp
from jax import lax
from jax.experimental import pallas as pl
from jax.experimental.pallas import tpu as pltpu
from jax.sharding import PartitionSpec as P

MESH = pl.DeviceIdType.MESH
F32 = jnp.float32
BF16 = jnp.bfloat16

TIME_STEP = 0.125
CAP = 48
LANES = 128
LEVELS = (2, 1, 0, 0, 1, 0, 0)


def dot(a, b):
    return lax.dot_general(a, b, (((1,), (0,)), ((), ())), preferred_element_type=F32)


def dot_nt(a, b):
    return lax.dot_general(a, b, (((1,), (1,)), ((), ())), preferred_element_type=F32)


def dot_full(a, b):
    return lax.dot_general(
        a, b, (((1,), (0,)), ((), ())), precision=lax.Precision.HIGHEST, preferred_element_type=F32
    )


def split2(x):
    hi = x.astype(BF16)
    return hi, (x - hi.astype(F32)).astype(BF16)


def split3(x):
    hi = x.astype(BF16)
    rest = x - hi.astype(F32)
    mid = rest.astype(BF16)
    return hi, mid, (rest - mid.astype(F32)).astype(BF16)


def left_pieces(x):
    hi, lo = split2(x)
    return jnp.concatenate([hi, lo, hi], axis=1)


def ones_where(mask):
    return jnp.where(mask, 1.0, 0.0).astype(BF16)


def kernel(
    n_slab,
    n_sub,
    adjoint_ref,
    scale_ref,
    cluster_ref,
    links_ref,
    list_ref,
    k_ref,
    self_ref,
    neighbour_ref,
    out_ref,
    x_ref,
    h_ref,
    q_ref,
    pt_ref,
    state_ref,
    factor_ref,
    linkb_ref,
    own_m_ref,
    halo_m_ref,
    g_own_ref,
    g_halo_ref,
    kk_ref,
    nn_ref,
    pad_ref,
    send_ref,
    recv_ref,
    id_send_ref,
    id_recv_ref,
    send_sem,
    recv_sem,
    id_send_sem,
    id_recv_sem,
):
    dofs, elems = adjoint_ref.shape
    side = elems // 4
    per = 4 * CAP
    slots = 3 * per

    i = lax.axis_index("slab")
    j = lax.axis_index("sub")
    low = ((i - 1, j), (i, j - 1))
    has_low = (i > 0, j > 0)
    high = ((i + 1, j), (i, j + 1))
    has_high = (i < n_slab - 1, j < n_sub - 1)
    target = (low[0], high[0], low[1], high[1])
    has_target = (has_low[0], has_high[0], has_low[1], has_high[1])
    has_source = (has_high[0], has_low[0], has_high[1], has_low[1])
    link_base = (elems + side, elems, elems + 3 * side, elems + 2 * side)

    barrier = pltpu.get_barrier_semaphore()
    for h in range(4):

        @pl.when(has_target[h])
        def _(h=h):
            pl.semaphore_signal(barrier, inc=1, device_id=target[h], device_id_type=MESH)

    def wave(k, h):
        return pltpu.make_async_remote_copy(
            src_ref=send_ref.at[k, pl.ds(h * CAP, CAP)],
            dst_ref=recv_ref.at[k, pl.ds(h * CAP, CAP)],
            send_sem=send_sem.at[k, h],
            recv_sem=recv_sem.at[k, h],
            device_id=target[h],
            device_id_type=MESH,
        )

    def id_wave(h):
        return pltpu.make_async_remote_copy(
            src_ref=id_send_ref,
            dst_ref=id_recv_ref.at[h],
            send_sem=id_send_sem.at[h],
            recv_sem=id_recv_sem.at[h],
            device_id=target[h],
            device_id_type=MESH,
        )

    def each_target(do):
        for h in range(4):

            @pl.when(has_target[h])
            def _(h=h):
                do(h)

    def each_source(do):
        for h in range(4):

            @pl.when(has_source[h])
            def _(h=h):
                do(h)

    listed = jnp.concatenate([list_ref[0:1, :], list_ref[1:2, :]], axis=1)
    h_ref[...] = ones_where(lax.broadcasted_iota(jnp.int32, (elems, elems), 0) == listed)

    cluster8 = jnp.broadcast_to(cluster_ref[...].astype(F32), (16, elems)).astype(BF16)
    cluster_p = dot(cluster8, h_ref[...])
    level_row = lax.broadcasted_iota(jnp.int32, (16, elems), 0).astype(F32)
    is_level = cluster_p == level_row
    before_from = lax.broadcasted_iota(jnp.int32, (elems, elems), 0)
    before_to = lax.broadcasted_iota(jnp.int32, (elems, elems), 1)
    before = ones_where((before_from < before_to) & (before_from // side == before_to // side))
    ranks = dot(ones_where(is_level), before)
    rank = jnp.sum(jnp.where(is_level, ranks, 0.0), axis=0, keepdims=True)
    position = lax.broadcasted_iota(jnp.int32, (1, elems), 1)
    slot = (cluster_p[0:1, :] * per + rank).astype(jnp.int32) + position // side * CAP
    q_ref[...] = ones_where(lax.broadcasted_iota(jnp.int32, (slots, elems), 0) == slot)

    side_of = position // side
    base = jnp.where(
        side_of == 0,
        link_base[0],
        jnp.where(side_of == 1, link_base[1], jnp.where(side_of == 2, link_base[2], link_base[3])),
    )
    own_plus = listed + 1
    far_plus = base + (position - side_of * side) + 1
    id_rows = jnp.concatenate(
        [
            (own_plus // 32 * 32).astype(F32),
            (own_plus % 32).astype(F32),
            (far_plus // 32 * 32).astype(F32),
            (far_plus % 32).astype(F32),
            jnp.zeros((12, elems), F32),
        ],
        axis=0,
    ).astype(BF16)
    own_ids = []
    for c in range(3):
        ids = dot_nt(id_rows, q_ref[c * per : (c + 1) * per, :])
        own = ids[0:1, :] + ids[1:2, :] - 1.0
        own_ids.append(jnp.concatenate([own, own], axis=1))
        far = ids[2:3, :] + ids[3:4, :] - 1.0
        id_send_ref[c : c + 1, :] = jnp.concatenate([far, far], axis=1)

    for h in range(4):

        @pl.when(jnp.logical_not(has_source[h]))
        def _(h=h):
            recv_ref[:, h * CAP : (h + 1) * CAP, :] = jnp.zeros((len(LEVELS), CAP, LANES), F32)
            id_recv_ref[h] = jnp.full(id_recv_ref.shape[1:], -1.0, F32)

    pl.semaphore_wait(barrier, sum(has.astype(jnp.int32) for has in has_target))
    each_target(lambda h: id_wave(h).start())

    x_ref[...] = jnp.zeros_like(x_ref)
    x_ref[0:dofs, :] = adjoint_ref[...]
    x_ref[dofs : dofs + 1, :] = scale_ref[...]
    x_ref[dofs + 1 : dofs + 5, :] = links_ref[...].astype(F32)
    moved = dot(jnp.concatenate(split3(x_ref[...]), axis=0), h_ref[...])
    moved = moved[0:LANES] + moved[LANES : 2 * LANES] + moved[2 * LANES :]
    moved3 = jnp.concatenate(split3(moved), axis=0)
    for c in (2, 1, 0):
        rows = slice(c * per, (c + 1) * per)
        placed = dot_nt(q_ref[rows, :], moved3)
        placed = placed[:, 0:LANES] + placed[:, LANES : 2 * LANES] + placed[:, 2 * LANES :]
        lane = lax.broadcasted_iota(jnp.int32, (per, LANES), 1)
        state_ref[rows, :] = jnp.where(lane < dofs, placed, 0.0)
        factor_ref[rows, :] = jnp.broadcast_to(placed[:, dofs : dofs + 1], (per, LANES))
        faces = [
            jnp.broadcast_to(placed[:, dofs + 1 + f : dofs + 2 + f], (per, LANES)) for f in range(4)
        ]
        for pair in range(2):
            first, second = faces[2 * pair], faces[2 * pair + 1]
            linkb_ref[3 * pair, rows, :] = first
            linkb_ref[3 * pair + 1, rows, :] = jnp.where(lane < LANES // 2, first, second)
            linkb_ref[3 * pair + 2, rows, :] = second

    pad_ref[...] = jnp.zeros_like(pad_ref)
    kk_ref[...] = jnp.zeros_like(kk_ref)
    pad_ref[0, 0:dofs, 0:dofs] = k_ref[...]
    pad_ref[1, 0:dofs, 0:dofs] = self_ref[...]
    for f in range(4):
        pad_ref[2 + f, 0:dofs, 0:dofs] = neighbour_ref[:, f * dofs : (f + 1) * dofs]

    def put(ref, at, matrix):
        hi, lo = split2(matrix)
        cols = slice(at * LANES, (at + 1) * LANES)
        ref[0:LANES, cols] = hi
        ref[LANES : 2 * LANES, cols] = hi
        ref[2 * LANES :, cols] = lo

    k1 = pad_ref[0].T
    k2 = dot_full(k1, k1)
    k3 = dot_full(k2, k1)
    for at, matrix in enumerate((k1, k2, k3)):
        put(kk_ref, at, matrix)
    for f in range(4):
        put(nn_ref, f, pad_ref[2 + f].T)
    put(nn_ref, 4, pad_ref[1].T)

    def step_size(c):
        return TIME_STEP * 2.0**c

    def rows_of(c):
        return slice(c * per, (c + 1) * per)

    def predict_and_send(k):
        c = LEVELS[k]
        v = state_ref[rows_of(c), :]
        terms = dot(left_pieces(v), kk_ref[...])
        a = step_size(c) * factor_ref[rows_of(c), :]
        w = (
            v
            + a * (1.0 / 2.0) * terms[:, 0:LANES]
            + a * a * (1.0 / 6.0) * terms[:, LANES : 2 * LANES]
            + a * a * a * (1.0 / 24.0) * terms[:, 2 * LANES :]
        )
        send_ref[k] = w
        each_target(lambda h: wave(k, h).start())

    def build(m_ref, c, ids):
        for block in range(6):
            row = ids[:, block % 3 * LANES : (block % 3 + 1) * LANES]
            m_ref[c, :, block * LANES : (block + 1) * LANES] = ones_where(linkb_ref[block] == row)

    def spread(g_ref, product):
        for f in range(4):
            hi, lo = split2(product[:, f * LANES : (f + 1) * LANES])
            g_ref[f * per : (f + 1) * per, 0:LANES] = hi
            g_ref[f * per : (f + 1) * per, LANES : 2 * LANES] = lo

    def gather(m_ref, g_ref, c, d):
        both = dot(m_ref[c, rows_of(d), :], g_ref[...])
        return both[:, 0:LANES] + both[:, LANES:]

    def add(c, d, change):
        a = step_size(c) * factor_ref[rows_of(d), :]
        state_ref[rows_of(d), :] += a * change

    seen = set()
    predict_and_send(0)
    each_source(lambda h: id_wave(h).wait_recv())
    for k, c in enumerate(LEVELS):
        if c not in seen:
            build(own_m_ref, c, own_ids[c])
        product = dot(left_pieces(send_ref[k]), nn_ref[...])
        spread(g_own_ref, product)
        for d in range(3):
            change = gather(own_m_ref, g_own_ref, c, d)
            if d == c:
                change = change + product[:, 4 * LANES :]
            add(c, d, change)
        if c not in seen:
            seen.add(c)
            lane = lax.broadcasted_iota(jnp.int32, (1, 2 * per), 1) % per
            ids = jnp.where(
                lane < CAP,
                id_recv_ref[0, c : c + 1, :],
                jnp.where(
                    lane < 2 * CAP,
                    id_recv_ref[1, c : c + 1, :],
                    jnp.where(lane < 3 * CAP, id_recv_ref[2, c : c + 1, :], id_recv_ref[3, c : c + 1, :]),
                ),
            )
            build(halo_m_ref, c, ids)
        if k == 0:
            pt_ref[...] = dot_nt(h_ref[...], q_ref[...]).astype(BF16)
        each_source(lambda h, k=k: wave(k, h).wait_recv())
        product = dot(left_pieces(recv_ref[k]), nn_ref[:, 0 : 4 * LANES])
        spread(g_halo_ref, product)
        order = [0, 1, 2]
        if k + 1 < len(LEVELS):
            order = [LEVELS[k + 1]] + [d for d in order if d != LEVELS[k + 1]]
        for at, d in enumerate(order):
            add(c, d, gather(halo_m_ref, g_halo_ref, c, d))
            if at == 0 and k + 1 < len(LEVELS):
                predict_and_send(k + 1)

    final = dot(pt_ref[...], jnp.concatenate(split3(state_ref[...]), axis=1))
    final = final[:, 0:LANES] + final[:, LANES : 2 * LANES] + final[:, 2 * LANES :]
    out_ref[...] = final.T[0:dofs, :]

    each_target(lambda h: id_wave(h).wait_send())
    for k in range(len(LEVELS)):
        each_target(lambda h, k=k: wave(k, h).wait_send())


def shards(n_slab, n_sub, adjoint, elem_scale, cluster, face_links, halo_list, k_matrix, w_self, w_neighbour):
    dofs, elems = adjoint.shape
    per = 4 * CAP
    slots = 3 * per
    count = len(LEVELS)
    vmem = pl.BlockSpec(memory_space=pltpu.VMEM)
    return pl.pallas_call(
        functools.partial(kernel, n_slab, n_sub),
        out_shape=jax.ShapeDtypeStruct((dofs, elems), F32),
        in_specs=[vmem] * 8,
        out_specs=vmem,
        scratch_shapes=[
            pltpu.VMEM((LANES, elems), F32),
            pltpu.VMEM((elems, elems), BF16),
            pltpu.VMEM((slots, elems), BF16),
            pltpu.VMEM((elems, slots), BF16),
            pltpu.VMEM((slots, LANES), F32),
            pltpu.VMEM((slots, LANES), F32),
            pltpu.VMEM((6, slots, LANES), F32),
            pltpu.VMEM((3, slots, 4 * per), BF16),
            pltpu.VMEM((3, slots, 4 * per), BF16),
            pltpu.VMEM((4 * per, 2 * LANES), BF16),
            pltpu.VMEM((4 * per, 2 * LANES), BF16),
            pltpu.VMEM((3 * LANES, 3 * LANES), BF16),
            pltpu.VMEM((3 * LANES, 5 * LANES), BF16),
            pltpu.VMEM((6, LANES, LANES), F32),
            pltpu.VMEM((count, per, LANES), F32),
            pltpu.VMEM((count, per, LANES), F32),
            pltpu.VMEM((8, 2 * per), F32),
            pltpu.VMEM((4, 8, 2 * per), F32),
            pltpu.SemaphoreType.DMA((count, 4)),
            pltpu.SemaphoreType.DMA((count, 4)),
            pltpu.SemaphoreType.DMA((4,)),
            pltpu.SemaphoreType.DMA((4,)),
        ],
        compiler_params=pltpu.CompilerParams(
            collective_id=0, has_side_effects=True, vmem_limit_bytes=40 * 1024 * 1024
        ),
    )(
        adjoint,
        elem_scale.reshape(1, elems),
        cluster.reshape(1, elems),
        face_links,
        halo_list,
        k_matrix,
        w_self,
        w_neighbour,
    )


def solution(mesh):
    placed = (
        P(None, ("slab", "sub")),
        P(("slab", "sub")),
        P(("slab", "sub")),
        P(None, ("slab", "sub")),
        P(None, ("slab", "sub")),
        P(),
        P(),
        P(),
    )
    return jax.shard_map(
        functools.partial(shards, mesh.shape["slab"], mesh.shape["sub"]),
        mesh=mesh,
        in_specs=placed,
        out_specs=P(None, ("slab", "sub")),
        check_vma=False,
    )
```

```python
import functools

import jax
import jax.numpy as jnp
from jax import lax
from jax.experimental import pallas as pl
from jax.experimental.pallas import tpu as pltpu
from jax.sharding import PartitionSpec as P

MESH = pl.DeviceIdType.MESH
F32 = jnp.float32
BF16 = jnp.bfloat16

TIME_STEP = 0.125
CAP = 48
LANES = 128
LEVELS = (2, 1, 0, 0, 1, 0, 0)


def dot(a, b):
    return lax.dot_general(a, b, (((1,), (0,)), ((), ())), preferred_element_type=F32)


def dot_nt(a, b):
    return lax.dot_general(a, b, (((1,), (1,)), ((), ())), preferred_element_type=F32)


def dot_full(a, b):
    return lax.dot_general(
        a, b, (((1,), (0,)), ((), ())), precision=lax.Precision.HIGHEST, preferred_element_type=F32
    )


def split2(x):
    hi = x.astype(BF16)
    return hi, (x - hi.astype(F32)).astype(BF16)


def left_pieces(x):
    hi, lo = split2(x)
    return jnp.concatenate([hi, lo, hi], axis=1)


def ones_where(mask):
    return jnp.where(mask, 1.0, 0.0).astype(BF16)


def kernel(
    n_slab,
    n_sub,
    adjoint_in,
    scale_in,
    cluster_in,
    links_in,
    list_in,
    k_in,
    self_in,
    neighbour_in,
    out_ref,
    adjoint_ref,
    scale_ref,
    cluster_ref,
    links_ref,
    list_ref,
    k_ref,
    self_ref,
    neighbour_ref,
    x_ref,
    h_ref,
    p_ref,
    state_ref,
    factor_ref,
    linkb_ref,
    own_m_ref,
    halo_m_ref,
    last_m_ref,
    g_own_ref,
    g_halo_ref,
    kk_ref,
    nn_ref,
    ns_ref,
    pad_ref,
    before_ref,
    pre_ref,
    send_ref,
    recv_ref,
    id_send_ref,
    id_recv_ref,
    in_sem,
    send_sem,
    recv_sem,
    id_send_sem,
    id_recv_sem,
):
    dofs, elems = adjoint_ref.shape
    side = elems // 4
    per = 4 * CAP
    half = per // 2
    slots = 3 * per
    count = len(LEVELS)

    def fetch(n, src, dst):
        copy = pltpu.make_async_copy(src, dst, in_sem.at[n])
        copy.start()
        return copy

    list_copy = fetch(0, list_in, list_ref)
    cluster_copy = fetch(1, cluster_in, cluster_ref)
    k_copy = fetch(2, k_in, k_ref)
    adjoint_copy = fetch(3, adjoint_in, adjoint_ref)
    scale_copy = fetch(4, scale_in, scale_ref)
    links_copy = fetch(5, links_in, links_ref)
    neighbour_copy = fetch(6, neighbour_in, neighbour_ref)
    self_copy = fetch(7, self_in, self_ref)

    i = lax.axis_index("slab")
    j = lax.axis_index("sub")
    low = ((i - 1, j), (i, j - 1))
    has_low = (i > 0, j > 0)
    high = ((i + 1, j), (i, j + 1))
    has_high = (i < n_slab - 1, j < n_sub - 1)
    target = (low[0], high[0], low[1], high[1])
    has_target = (has_low[0], has_high[0], has_low[1], has_high[1])
    has_source = (has_high[0], has_low[0], has_high[1], has_low[1])
    link_base = (elems + side, elems, elems + 3 * side, elems + 2 * side)

    barrier = pltpu.get_barrier_semaphore()
    for h in range(4):

        @pl.when(has_target[h])
        def _(h=h):
            pl.semaphore_signal(barrier, inc=1, device_id=target[h], device_id_type=MESH)

    def wave(k, h):
        return pltpu.make_async_remote_copy(
            src_ref=send_ref.at[k, pl.ds(h * CAP, CAP)],
            dst_ref=recv_ref.at[k, pl.ds(h * CAP, CAP)],
            send_sem=send_sem.at[k, h],
            recv_sem=recv_sem.at[k, h],
            device_id=target[h],
            device_id_type=MESH,
        )

    def id_wave(c, h):
        return pltpu.make_async_remote_copy(
            src_ref=id_send_ref.at[c],
            dst_ref=id_recv_ref.at[c, h],
            send_sem=id_send_sem.at[c, h],
            recv_sem=id_recv_sem.at[c, h],
            device_id=target[h],
            device_id_type=MESH,
        )

    def each(has, do, sides=(2, 3, 0, 1)):
        for h in sides:

            @pl.when(has[h])
            def _(h=h):
                do(h)

    for h in range(4):

        @pl.when(jnp.logical_not(has_source[h]))
        def _(h=h):
            recv_ref[:, h * CAP : (h + 1) * CAP, :] = jnp.zeros((count, CAP, LANES), F32)
            id_recv_ref[:, h] = jnp.full((3,) + id_recv_ref.shape[2:], -1.0, F32)

    before_from = lax.broadcasted_iota(jnp.int32, (elems, elems), 0)
    before_to = lax.broadcasted_iota(jnp.int32, (elems, elems), 1)
    before_ref[...] = ones_where(
        (before_from < before_to) & (before_from // side == before_to // side)
    )
    pad_ref[...] = jnp.zeros_like(pad_ref)
    kk_ref[...] = jnp.zeros_like(kk_ref)
    x_ref[...] = jnp.zeros_like(x_ref)
    id_send_ref[...] = jnp.full(id_send_ref.shape, -1.0, F32)
    state_ref[slots:, :] = jnp.zeros((state_ref.shape[0] - slots, LANES), F32)
    p_ref[slots:, :] = jnp.zeros((p_ref.shape[0] - slots, elems), BF16)

    list_copy.wait()
    cluster_copy.wait()
    k_copy.wait()
    adjoint_copy.wait()
    scale_copy.wait()
    links_copy.wait()

    listed = jnp.concatenate([list_ref[0:1, :], list_ref[1:2, :]], axis=1)
    h_ref[...] = ones_where(lax.broadcasted_iota(jnp.int32, (elems, elems), 0) == listed)

    cluster8 = jnp.broadcast_to(cluster_ref[...].astype(F32), (16, elems)).astype(BF16)
    cluster_p = dot(cluster8, h_ref[...])
    level_row = lax.broadcasted_iota(jnp.int32, (16, elems), 0).astype(F32)
    is_level = cluster_p == level_row
    ranks = dot(ones_where(is_level), before_ref[...])
    rank = jnp.sum(jnp.where(is_level, ranks, 0.0), axis=0, keepdims=True)
    position = lax.broadcasted_iota(jnp.int32, (1, elems), 1)
    side_of = position // side
    slot = (cluster_p[0:1, :] * per + rank).astype(jnp.int32) + side_of * CAP

    base = jnp.where(
        side_of == 0,
        link_base[0],
        jnp.where(side_of == 1, link_base[1], jnp.where(side_of == 2, link_base[2], link_base[3])),
    )
    own_plus = listed + 1
    far_plus = base + (position - side_of * side) + 1
    id_rows = jnp.concatenate(
        [
            (own_plus // 32 * 32).astype(F32),
            (own_plus % 32).astype(F32),
            (far_plus // 32 * 32).astype(F32),
            (far_plus % 32).astype(F32),
            jnp.zeros((12, elems), F32),
        ],
        axis=0,
    ).astype(BF16)

    def step_size(c):
        return TIME_STEP * 2.0**c

    def rows_of(c):
        return slice(c * per, (c + 1) * per)

    aux = jnp.concatenate(
        [scale_ref[...], links_ref[...].astype(F32), jnp.zeros((11, elems), F32)], axis=0
    )
    for at, part in ((0, adjoint_ref[...]), (dofs, aux)):
        hi, lo = split2(part)
        x_ref[at : at + part.shape[0], :] = hi
        x_ref[LANES + at : LANES + at + part.shape[0], :] = lo

    own_ids = {}

    def place(c):
        rows = rows_of(c)
        q = ones_where(lax.broadcasted_iota(jnp.int32, (per, elems), 0) + c * per == slot)
        ids = dot_nt(id_rows, q)
        own = ids[0:1, :] + ids[1:2, :] - 1.0
        own_ids[c] = jnp.concatenate([own, own], axis=1)
        id_send_ref[c, 0:1, 0:per] = ids[2:3, :] + ids[3:4, :] - 1.0
        p = dot_nt(q, h_ref[...]).astype(BF16)
        p_ref[rows, :] = p
        placed = dot_nt(p, x_ref[...])
        placed = placed[:, 0:LANES] + placed[:, LANES:]
        lane = lax.broadcasted_iota(jnp.int32, (per, LANES), 1)
        state_ref[rows, :] = jnp.where(lane < dofs, placed, 0.0)
        factor_ref[rows, :] = jnp.broadcast_to(placed[:, dofs : dofs + 1], (per, LANES))
        return placed

    def spread_links(c, placed):
        rows = rows_of(c)
        lane = lax.broadcasted_iota(jnp.int32, (per, LANES), 1)
        faces = [
            jnp.broadcast_to(placed[:, dofs + 1 + f : dofs + 2 + f], (per, LANES)) for f in range(4)
        ]
        linkb_ref[0, rows, :] = faces[0]
        linkb_ref[1, rows, :] = jnp.where(lane < LANES // 2, faces[0], faces[1])
        linkb_ref[2, rows, :] = faces[1]
        linkb_ref[3, rows, :] = faces[2]
        linkb_ref[4, rows, :] = jnp.where(lane < LANES // 2, faces[2], faces[3])
        linkb_ref[5, rows, :] = faces[3]
        for block in range(3):
            cut = half - block * (LANES - half)
            linkb_ref[6 + block, rows, :] = jnp.where(lane < cut, faces[block], faces[block + 1])

    def put(ref, at, matrix):
        hi, lo = split2(matrix)
        cols = slice(at * LANES, (at + 1) * LANES)
        ref[0:LANES, cols] = hi
        ref[LANES : 2 * LANES, cols] = hi
        ref[2 * LANES :, cols] = lo

    pad_ref[0, 0:dofs, 0:dofs] = k_ref[...]
    k1 = pad_ref[0].T
    k2 = dot_full(k1, k1)
    k3 = dot_full(k2, k1)
    for at, matrix in enumerate((k1, k2, k3)):
        put(kk_ref, at, matrix)

    def predict(k):
        c = LEVELS[k]
        v = state_ref[rows_of(c), :]
        terms = dot(left_pieces(v), kk_ref[...])
        a = step_size(c) * factor_ref[rows_of(c), :]
        send_ref[k] = (
            v
            + a * (1.0 / 2.0) * terms[:, 0:LANES]
            + a * a * (1.0 / 6.0) * terms[:, LANES : 2 * LANES]
            + a * a * a * (1.0 / 24.0) * terms[:, 2 * LANES :]
        )

    def send(k):
        each(has_target, lambda h: wave(k, h).start())

    def build(m_ref, c, col, links_at, blocks, ids):
        for block in range(blocks):
            row = ids[:, block % 3 * LANES : (block % 3 + 1) * LANES]
            at = (col + block) * LANES
            m_ref[c, :, at : at + LANES] = ones_where(linkb_ref[links_at + block, 0:slots, :] == row)

    def spread(g_ref, at, product):
        size = product.shape[0]
        for f in range(4):
            hi, lo = split2(product[:, f * LANES : (f + 1) * LANES])
            rows = slice(at + f * size, at + (f + 1) * size)
            g_ref[rows, 0:LANES] = hi
            g_ref[rows, LANES : 2 * LANES] = lo

    def gather(m, g):
        both = dot(m, g)
        return both[:, 0:LANES] + both[:, LANES:]

    def add(c, d, change):
        a = step_size(c) * factor_ref[rows_of(d), :]
        state_ref[rows_of(d), :] += a * change

    def halo_ids(c):
        lane = lax.broadcasted_iota(jnp.int32, (1, 2 * LANES), 1)
        ids = [id_recv_ref[c, h, 0:1, :] for h in range(4)]
        return jnp.where(
            lane < CAP,
            ids[0],
            jnp.where(lane < 2 * CAP, ids[1], jnp.where(lane < 3 * CAP, ids[2], ids[3])),
        )

    first = LEVELS[0]
    placed = {first: place(first)}
    predict(0)
    pl.semaphore_wait(barrier, sum(has.astype(jnp.int32) for has in has_target))
    each(has_target, lambda h: id_wave(first, h).start())
    send(0)

    for c in (1, 0):
        placed[c] = place(c)
    each(has_target, lambda h: id_wave(1, h).start())
    each(has_target, lambda h: id_wave(0, h).start())
    for c in (2, 1, 0):
        spread_links(c, placed[c])

    neighbour_copy.wait()
    self_copy.wait()
    pad_ref[1, 0:dofs, 0:dofs] = self_ref[...]
    for f in range(4):
        pad_ref[2 + f, 0:dofs, 0:dofs] = neighbour_ref[:, f * dofs : (f + 1) * dofs]
    for f in range(4):
        put(nn_ref, f, pad_ref[2 + f].T)
        hi, lo = split2(pad_ref[2 + f, 0:dofs, :])
        ns_ref[f * dofs : (f + 1) * dofs, :] = jnp.concatenate([hi, hi, lo], axis=1)
    put(nn_ref, 4, pad_ref[1].T)

    seen = set()
    for k, c in enumerate(LEVELS):
        last = k == count - 1
        if c not in seen:
            build(own_m_ref, c, 0, 0, 6, own_ids[c])
        product = dot(left_pieces(send_ref[k]), nn_ref[...])
        spread(g_own_ref, 0, product)
        for d in range(3):
            change = gather(own_m_ref[c, rows_of(d), :], g_own_ref[...])
            if d == c:
                change = change + product[:, 4 * LANES :]
            add(c, d, change)
        if c not in seen:
            seen.add(c)
            each(has_source, lambda h, c=c: id_wave(c, h).wait_recv())
            ids = halo_ids(c)
            for part in range(2):
                cut = ids[:, part * half : (part + 1) * half]
                build(halo_m_ref, c, 3 * part, 6, 3, jnp.concatenate([cut] * 4, axis=1))
        if last:
            ids = halo_ids(c)
            for block in range(2):
                size = min(LANES, per - block * LANES)
                row = ids[:, block * LANES : (block + 1) * LANES]
                column = jnp.broadcast_to(row, (LANES, LANES)).T
                column = jnp.concatenate([column] * 4, axis=1)[0:size, :]
                for f in range(4):
                    row = links_ref[f : f + 1, :].astype(F32)
                    last_m_ref[f, block * LANES : block * LANES + size, :] = ones_where(column == row)
            turned = jnp.concatenate(
                [state_ref[at * LANES : (at + 1) * LANES, :].T for at in range(5)], axis=1
            )
            both = dot(jnp.concatenate(split2(turned), axis=0), p_ref[...])
            pre_ref[...] = (both[0:LANES] + both[LANES:])[0:dofs, :]
            each(has_source, lambda h, k=k: wave(k, h).wait_recv())
            product = dot_nt(ns_ref[...], left_pieces(recv_ref[k]))
            total = jnp.zeros((2 * dofs, elems), F32)
            for f in range(4):
                pieces = split2(product[f * dofs : (f + 1) * dofs, :])
                total = total + dot(jnp.concatenate(pieces, axis=0), last_m_ref[f])
            a = step_size(c) * scale_ref[...]
            out_ref[...] = pre_ref[...] + a * (total[0:dofs] + total[dofs:])
        else:
            then = LEVELS[k + 1]
            rest = [d for d in range(3) if d != then]
            wide = 2 * per
            each(has_source, lambda h, k=k: wave(k, h).wait_recv(), (0, 1))
            product = dot(left_pieces(recv_ref[k, 0:half, :]), nn_ref[:, 0 : 4 * LANES])
            spread(g_halo_ref, 0, product)
            add(c, then, gather(halo_m_ref[c, rows_of(then), 0:wide], g_halo_ref[0:wide, :]))
            each(has_source, lambda h, k=k: wave(k, h).wait_recv(), (2, 3))
            product = dot(left_pieces(recv_ref[k, half:per, :]), nn_ref[:, 0 : 4 * LANES])
            spread(g_halo_ref, wide, product)
            add(c, then, gather(halo_m_ref[c, rows_of(then), wide:], g_halo_ref[wide:, :]))
            predict(k + 1)
            send(k + 1)
            for d in rest:
                add(c, d, gather(halo_m_ref[c, rows_of(d), :], g_halo_ref[...]))

    for c in range(3):
        each(has_target, lambda h, c=c: id_wave(c, h).wait_send())
    for k in range(count):
        each(has_target, lambda h, k=k: wave(k, h).wait_send())


def shards(n_slab, n_sub, adjoint, elem_scale, cluster, face_links, halo_list, k_matrix, w_self, w_neighbour):
    dofs, elems = adjoint.shape
    per = 4 * CAP
    slots = 3 * per
    padded = 5 * LANES
    count = len(LEVELS)
    operands = (
        adjoint,
        elem_scale.reshape(1, elems),
        cluster.reshape(1, elems),
        face_links,
        halo_list,
        k_matrix,
        w_self,
        w_neighbour,
    )
    return pl.pallas_call(
        functools.partial(kernel, n_slab, n_sub),
        out_shape=jax.ShapeDtypeStruct((dofs, elems), F32),
        in_specs=[pl.BlockSpec(memory_space=pltpu.HBM)] * 8,
        out_specs=pl.BlockSpec(memory_space=pltpu.VMEM),
        scratch_shapes=[pltpu.VMEM(x.shape, x.dtype) for x in operands]
        + [
            pltpu.VMEM((2 * LANES, elems), BF16),
            pltpu.VMEM((elems, elems), BF16),
            pltpu.VMEM((padded, elems), BF16),
            pltpu.VMEM((padded, LANES), F32),
            pltpu.VMEM((slots, LANES), F32),
            pltpu.VMEM((9, slots, LANES), F32),
            pltpu.VMEM((3, slots, 4 * per), BF16),
            pltpu.VMEM((3, slots, 4 * per), BF16),
            pltpu.VMEM((4, per, elems), BF16),
            pltpu.VMEM((4 * per, 2 * LANES), BF16),
            pltpu.VMEM((4 * per, 2 * LANES), BF16),
            pltpu.VMEM((3 * LANES, 3 * LANES), BF16),
            pltpu.VMEM((3 * LANES, 5 * LANES), BF16),
            pltpu.VMEM((4 * dofs, 3 * LANES), BF16),
            pltpu.VMEM((6, LANES, LANES), F32),
            pltpu.VMEM((elems, elems), BF16),
            pltpu.VMEM((dofs, elems), F32),
            pltpu.VMEM((count, per, LANES), F32),
            pltpu.VMEM((count, per, LANES), F32),
            pltpu.VMEM((3, 8, 2 * LANES), F32),
            pltpu.VMEM((3, 4, 8, 2 * LANES), F32),
            pltpu.SemaphoreType.DMA((8,)),
            pltpu.SemaphoreType.DMA((count, 4)),
            pltpu.SemaphoreType.DMA((count, 4)),
            pltpu.SemaphoreType.DMA((3, 4)),
            pltpu.SemaphoreType.DMA((3, 4)),
        ],
        compiler_params=pltpu.CompilerParams(
            collective_id=0, has_side_effects=True, vmem_limit_bytes=58 * 1024 * 1024
        ),
    )(*operands)


def solution(mesh):
    placed = (
        P(None, ("slab", "sub")),
        P(("slab", "sub")),
        P(("slab", "sub")),
        P(None, ("slab", "sub")),
        P(None, ("slab", "sub")),
        P(),
        P(),
        P(),
    )
    return jax.shard_map(
        functools.partial(shards, mesh.shape["slab"], mesh.shape["sub"]),
        mesh=mesh,
        in_specs=placed,
        out_specs=P(None, ("slab", "sub")),
        check_vma=False,
    )
```

```python
import functools

import jax
import jax.numpy as jnp
from jax import lax
from jax.experimental import pallas as pl
from jax.experimental.pallas import tpu as pltpu
from jax.sharding import PartitionSpec as P

MESH = pl.DeviceIdType.MESH
F32 = jnp.float32
BF16 = jnp.bfloat16

TIME_STEP = 0.125
CAP = 48
LANES = 128
PACKED = 32
SPARE = CAP - PACKED
LEVELS = (2, 1, 0, 0, 1, 0, 0)


def dot(a, b):
    return lax.dot_general(a, b, (((1,), (0,)), ((), ())), preferred_element_type=F32)


def dot_nt(a, b):
    return lax.dot_general(a, b, (((1,), (1,)), ((), ())), preferred_element_type=F32)


def dot_full(a, b):
    return lax.dot_general(
        a, b, (((1,), (0,)), ((), ())), precision=lax.Precision.HIGHEST, preferred_element_type=F32
    )


def split2(x):
    hi = x.astype(BF16)
    return hi, (x - hi.astype(F32)).astype(BF16)


def left_pieces(x):
    hi, lo = split2(x)
    return jnp.concatenate([hi, lo, hi], axis=1)


def ones_where(mask):
    return jnp.where(mask, 1.0, 0.0).astype(BF16)


def kernel(
    n_slab,
    n_sub,
    adjoint_in,
    scale_in,
    cluster_in,
    links_in,
    list_in,
    k_in,
    self_in,
    neighbour_in,
    out_ref,
    adjoint_ref,
    scale_ref,
    cluster_ref,
    links_ref,
    list_ref,
    k_ref,
    self_ref,
    neighbour_ref,
    x_ref,
    moved_ref,
    h_ref,
    q_ref,
    p_ref,
    state_ref,
    factor_ref,
    powers_ref,
    linkb_ref,
    own_m_ref,
    halo_m_ref,
    last_m_ref,
    g_own_ref,
    g_halo_ref,
    kk_ref,
    nn_ref,
    ns_ref,
    pad_ref,
    before_ref,
    pre_ref,
    send_ref,
    pack_ref,
    recv_ref,
    id_send_ref,
    id_recv_ref,
    in_sem,
    send_sem,
    recv_sem,
    id_send_sem,
    id_recv_sem,
):
    dofs, elems = adjoint_ref.shape
    side = elems // 4
    per = 4 * CAP
    half = per // 2
    slots = 3 * per
    count = len(LEVELS)

    def fetch(n, src, dst):
        copy = pltpu.make_async_copy(src, dst, in_sem.at[n])
        copy.start()
        return copy

    list_copy = fetch(0, list_in, list_ref)
    cluster_copy = fetch(1, cluster_in, cluster_ref)
    k_copy = fetch(2, k_in, k_ref)
    adjoint_copy = fetch(3, adjoint_in, adjoint_ref)
    scale_copy = fetch(4, scale_in, scale_ref)
    links_copy = fetch(5, links_in, links_ref)
    neighbour_copy = fetch(6, neighbour_in, neighbour_ref)
    self_copy = fetch(7, self_in, self_ref)

    i = lax.axis_index("slab")
    j = lax.axis_index("sub")
    low = ((i - 1, j), (i, j - 1))
    has_low = (i > 0, j > 0)
    high = ((i + 1, j), (i, j + 1))
    has_high = (i < n_slab - 1, j < n_sub - 1)
    target = (low[0], high[0], low[1], high[1])
    has_target = (has_low[0], has_high[0], has_low[1], has_high[1])
    has_source = (has_high[0], has_low[0], has_high[1], has_low[1])
    link_base = (elems + side, elems, elems + 3 * side, elems + 2 * side)

    barrier = pltpu.get_barrier_semaphore()
    for h in range(4):

        @pl.when(has_target[h])
        def _(h=h):
            pl.semaphore_signal(barrier, inc=1, device_id=target[h], device_id_type=MESH)

    def wave(k, h):
        at = pl.ds(h * PACKED, PACKED)
        return pltpu.make_async_remote_copy(
            src_ref=pack_ref.at[k, at],
            dst_ref=recv_ref.at[k, at],
            send_sem=send_sem.at[h],
            recv_sem=recv_sem.at[k % 2, h],
            device_id=target[h],
            device_id_type=MESH,
        )

    def id_wave(c, h):
        return pltpu.make_async_remote_copy(
            src_ref=id_send_ref.at[c],
            dst_ref=id_recv_ref.at[c, h],
            send_sem=id_send_sem.at[c, h],
            recv_sem=id_recv_sem.at[c, h],
            device_id=target[h],
            device_id_type=MESH,
        )

    def each(has, do, sides=(2, 3, 0, 1)):
        for h in sides:

            @pl.when(has[h])
            def _(h=h):
                do(h)

    for h in range(4):

        @pl.when(jnp.logical_not(has_source[h]))
        def _(h=h):
            recv_ref[:, h * PACKED : (h + 1) * PACKED, :] = jnp.zeros((count, PACKED, LANES), F32)
            id_recv_ref[:, h] = jnp.full((3,) + id_recv_ref.shape[2:], -1.0, F32)

    before_from = lax.broadcasted_iota(jnp.int32, (2 * side, 2 * side), 0)
    before_to = lax.broadcasted_iota(jnp.int32, (2 * side, 2 * side), 1)
    before_ref[...] = ones_where(
        (before_from < before_to) & (before_from // side == before_to // side)
    )
    pad_ref[...] = jnp.zeros_like(pad_ref)
    kk_ref[...] = jnp.zeros_like(kk_ref)
    x_ref[...] = jnp.zeros_like(x_ref)
    id_send_ref[...] = jnp.full(id_send_ref.shape, -1.0, F32)
    state_ref[slots:, :] = jnp.zeros((state_ref.shape[0] - slots, LANES), F32)
    p_ref[slots:, :] = jnp.zeros((p_ref.shape[0] - slots, elems), BF16)

    list_copy.wait()
    cluster_copy.wait()
    k_copy.wait()
    adjoint_copy.wait()
    scale_copy.wait()
    links_copy.wait()

    listed = jnp.concatenate([list_ref[0:1, :], list_ref[1:2, :]], axis=1)
    h_ref[...] = ones_where(lax.broadcasted_iota(jnp.int32, (elems, elems), 0) == listed)

    aux = jnp.concatenate(
        [scale_ref[...], links_ref[...].astype(F32), jnp.zeros((11, elems), F32)], axis=0
    )
    for at, part in ((0, adjoint_ref[...]), (dofs, aux)):
        hi, lo = split2(part)
        x_ref[at : at + part.shape[0], :] = hi
        x_ref[LANES + at : LANES + at + part.shape[0], :] = lo

    cluster8 = jnp.broadcast_to(cluster_ref[...].astype(F32), (16, elems)).astype(BF16)
    by_position = dot(jnp.concatenate([cluster8, x_ref[...]], axis=0), h_ref[...])
    cluster_p = by_position[0:16, :]
    moved_ref[...] = by_position[16:, :].astype(BF16)

    level_row = lax.broadcasted_iota(jnp.int32, (16, elems), 0).astype(F32)
    is_level = cluster_p == level_row
    marks = ones_where(is_level)
    ranks = jnp.concatenate(
        [dot(marks[:, 0 : 2 * side], before_ref[...]), dot(marks[:, 2 * side :], before_ref[...])],
        axis=1,
    )
    rank = jnp.sum(jnp.where(is_level, ranks, 0.0), axis=0, keepdims=True)
    position = lax.broadcasted_iota(jnp.int32, (1, elems), 1)
    side_of = position // side
    rank = rank.astype(jnp.int32)
    within = jnp.where(
        rank < PACKED, 4 * SPARE + side_of * PACKED + rank, side_of * SPARE + rank - PACKED
    )
    slot = cluster_p[0:1, :].astype(jnp.int32) * per + within

    base = jnp.where(
        side_of == 0,
        link_base[0],
        jnp.where(side_of == 1, link_base[1], jnp.where(side_of == 2, link_base[2], link_base[3])),
    )
    own_plus = listed + 1
    far_plus = base + (position - side_of * side) + 1
    id_rows = jnp.concatenate(
        [
            (own_plus // 32 * 32).astype(F32),
            (own_plus % 32).astype(F32),
            (far_plus // 32 * 32).astype(F32),
            (far_plus % 32).astype(F32),
            jnp.zeros((12, elems), F32),
        ],
        axis=0,
    ).astype(BF16)

    def step_size(c):
        return TIME_STEP * 2.0**c

    def rows_of(c):
        return slice(c * per, (c + 1) * per)

    own_ids = {}

    def place(c):
        rows = rows_of(c)
        q = ones_where(lax.broadcasted_iota(jnp.int32, (per, elems), 0) + c * per == slot)
        ids = dot_nt(id_rows, q)
        own = ids[0:1, :] + ids[1:2, :] - 1.0
        own_ids[c] = jnp.concatenate([own, own], axis=1)
        id_send_ref[c, :, 0:per] = ids[2:3, :] + ids[3:4, :] - 1.0
        q_ref[rows, :] = q
        placed = dot_nt(q, moved_ref[...])
        placed = placed[:, 0:LANES] + placed[:, LANES:]
        lane = lax.broadcasted_iota(jnp.int32, (per, LANES), 1)
        state_ref[rows, :] = jnp.where(lane < dofs, placed, 0.0)
        factor = jnp.broadcast_to(placed[:, dofs : dofs + 1], (per, LANES))
        factor_ref[rows, :] = factor
        a = step_size(c) * factor
        powers_ref[0, rows, :] = a * (1.0 / 2.0)
        powers_ref[1, rows, :] = a * a * (1.0 / 6.0)
        powers_ref[2, rows, :] = a * a * a * (1.0 / 24.0)
        return placed

    def spread_links(c, placed):
        rows = rows_of(c)
        lane = lax.broadcasted_iota(jnp.int32, (per, LANES), 1)
        faces = [
            jnp.broadcast_to(placed[:, dofs + 1 + f : dofs + 2 + f], (per, LANES)) for f in range(4)
        ]
        linkb_ref[0, rows, :] = faces[0]
        linkb_ref[1, rows, :] = jnp.where(lane < LANES // 2, faces[0], faces[1])
        linkb_ref[2, rows, :] = faces[1]
        linkb_ref[3, rows, :] = faces[2]
        linkb_ref[4, rows, :] = jnp.where(lane < LANES // 2, faces[2], faces[3])
        linkb_ref[5, rows, :] = faces[3]
        for block in range(3):
            cut = half - block * (LANES - half)
            linkb_ref[6 + block, rows, :] = jnp.where(lane < cut, faces[block], faces[block + 1])

    def put(ref, at, matrix):
        hi, lo = split2(matrix)
        cols = slice(at * LANES, (at + 1) * LANES)
        ref[0:LANES, cols] = hi
        ref[LANES : 2 * LANES, cols] = hi
        ref[2 * LANES :, cols] = lo

    pad_ref[0, 0:dofs, 0:dofs] = k_ref[...]
    k1 = pad_ref[0].T
    k2 = dot_full(k1, k1)
    k3 = dot_full(k2, k1)
    for at, matrix in enumerate((k1, k2, k3)):
        put(kk_ref, at, matrix)

    def predict(k):
        c = LEVELS[k]
        rows = rows_of(c)
        v = state_ref[rows, :]
        terms = dot(left_pieces(v), kk_ref[...])
        w = v
        for n in range(3):
            w = w + powers_ref[n, rows, :] * terms[:, n * LANES : (n + 1) * LANES]
        send_ref[k] = w
        lane = lax.broadcasted_iota(jnp.int32, (SPARE, LANES), 1)
        for h in range(4):
            bottom = w[h * SPARE : (h + 1) * SPARE]
            for m, shift in enumerate((dofs, dofs - CAP)):
                at = h * PACKED + m * SPARE
                top = w[4 * SPARE + at : 4 * SPARE + at + SPARE]
                pack_ref[k, at : at + SPARE, :] = jnp.where(
                    lane < dofs, top, pltpu.roll(bottom, shift, 1)
                )

    def unpacked(k, sides):
        lane = lax.broadcasted_iota(jnp.int32, (SPARE, LANES), 1)
        rows = [recv_ref[k, sides[0] * PACKED : (sides[-1] + 1) * PACKED, :]]
        for h in sides:
            first = recv_ref[k, h * PACKED : h * PACKED + SPARE, :]
            second = recv_ref[k, h * PACKED + SPARE : (h + 1) * PACKED, :]
            rows.append(
                jnp.where(
                    lane < LANES - dofs,
                    pltpu.roll(first, LANES - dofs, 1),
                    pltpu.roll(second, LANES - dofs + CAP, 1),
                )
            )
        return jnp.concatenate(rows, axis=0)

    even = lax.rem(i, 2) == 0
    off_chip = tuple(jnp.logical_and(has_target[h], even if h == 0 else jnp.logical_not(even)) for h in range(2))
    on_chip = tuple(jnp.logical_and(has_target[h], jnp.logical_not(even) if h == 0 else even) for h in range(2))

    def send(k):
        start = lambda h: wave(k, h).start()
        each(off_chip, start, (1,))
        each(has_target, start, (2, 3))
        each(off_chip, start, (0,))
        each(on_chip, start, (0, 1))

    def build(m_ref, c, col, links_at, blocks, ids):
        for block in range(blocks):
            row = ids[:, block % 3 * LANES : (block % 3 + 1) * LANES]
            at = (col + block) * LANES
            m_ref[c, :, at : at + LANES] = ones_where(linkb_ref[links_at + block, 0:slots, :] == row)

    def spread(g_ref, at, product):
        size = product.shape[0]
        for f in range(4):
            hi, lo = split2(product[:, f * LANES : (f + 1) * LANES])
            rows = slice(at + f * size, at + (f + 1) * size)
            g_ref[rows, 0:LANES] = hi
            g_ref[rows, LANES : 2 * LANES] = lo

    def gather(m, g):
        both = dot(m, g)
        return both[:, 0:LANES] + both[:, LANES:]

    def add(c, rows, change):
        state_ref[rows, :] += step_size(c) * factor_ref[rows, :] * change

    def halo_ids(c):
        lane = lax.broadcasted_iota(jnp.int32, (1, 2 * LANES), 1)
        side_at = jnp.where(lane < 4 * SPARE, lane // SPARE, (lane - 4 * SPARE) // PACKED)
        ids = [id_recv_ref[c, h] for h in range(4)]
        return jnp.where(
            side_at == 0,
            ids[0],
            jnp.where(side_at == 1, ids[1], jnp.where(side_at == 2, ids[2], ids[3])),
        )

    first = LEVELS[0]
    placed = {first: place(first)}
    predict(0)
    pl.semaphore_wait(barrier, sum(has.astype(jnp.int32) for has in has_target))
    each(has_target, lambda h: id_wave(first, h).start())
    send(0)

    for c in (1, 0):
        placed[c] = place(c)
    each(has_target, lambda h: id_wave(1, h).start())
    each(has_target, lambda h: id_wave(0, h).start())
    for c in (2, 1, 0):
        spread_links(c, placed[c])

    neighbour_copy.wait()
    self_copy.wait()
    pad_ref[1, 0:dofs, 0:dofs] = self_ref[...]
    for f in range(4):
        pad_ref[2 + f, 0:dofs, 0:dofs] = neighbour_ref[:, f * dofs : (f + 1) * dofs]
    for f in range(4):
        put(nn_ref, f, pad_ref[2 + f].T)
        hi, lo = split2(pad_ref[2 + f, 0:dofs, :])
        ns_ref[f * dofs : (f + 1) * dofs, :] = jnp.concatenate([hi, hi, lo], axis=1)
    put(nn_ref, 4, pad_ref[1].T)

    seen = set()
    for k, c in enumerate(LEVELS):
        last = k == count - 1
        if c not in seen:
            build(own_m_ref, c, 0, 0, 6, own_ids[c])
        product = dot(left_pieces(send_ref[k]), nn_ref[...])
        spread(g_own_ref, 0, product)
        for d in range(3):
            change = gather(own_m_ref[c, rows_of(d), :], g_own_ref[...])
            if d == c:
                change = change + product[:, 4 * LANES :]
            add(c, rows_of(d), change)
        if c not in seen:
            seen.add(c)
            each(has_source, lambda h, c=c: id_wave(c, h).wait_recv())
            ids = halo_ids(c)
            for part in range(2):
                tops = 4 * SPARE + 2 * part * PACKED
                cut = [
                    ids[:, tops : tops + 2 * PACKED],
                    ids[:, 2 * part * SPARE : 2 * (part + 1) * SPARE],
                ]
                build(halo_m_ref, c, 3 * part, 6, 3, jnp.concatenate(cut * 4, axis=1))
        each(has_target, lambda h, k=k: wave(k, h).wait_send())
        if k in (1, 2, 3):
            each(has_target, lambda h, k=k: id_wave(k - 1, h).wait_send())
        if k == 3:
            p_ref[0:slots, :] = dot_nt(q_ref[...], h_ref[...]).astype(BF16)
        if last:
            ids = halo_ids(c)
            for block in range(2):
                size = min(LANES, per - block * LANES)
                at = 4 * SPARE * (1 - block)
                row = ids[:, at : at + LANES]
                column = jnp.broadcast_to(row, (LANES, LANES)).T
                column = jnp.concatenate([column] * 4, axis=1)[0:size, :]
                for f in range(4):
                    row = links_ref[f : f + 1, :].astype(F32)
                    last_m_ref[f, block * LANES : block * LANES + size, :] = ones_where(column == row)
            turned = jnp.concatenate(
                [state_ref[at * LANES : (at + 1) * LANES, :].T for at in range(5)], axis=1
            )
            both = dot(jnp.concatenate(split2(turned), axis=0), p_ref[...])
            pre_ref[...] = (both[0:LANES] + both[LANES:])[0:dofs, :]
            each(has_source, lambda h, k=k: wave(k, h).wait_recv())
            got = unpacked(k, (0, 1, 2, 3))
            product = dot_nt(ns_ref[...], left_pieces(got))
            total = jnp.zeros((2 * dofs, elems), F32)
            for f in range(4):
                pieces = split2(product[f * dofs : (f + 1) * dofs, :])
                total = total + dot(jnp.concatenate(pieces, axis=0), last_m_ref[f])
            a = step_size(c) * scale_ref[...]
            out_ref[...] = pre_ref[...] + a * (total[0:dofs] + total[dofs:])
        else:
            then = LEVELS[k + 1]
            rest = [d for d in range(3) if d != then]
            wide = 2 * per
            for part, sides in enumerate(((0, 1), (2, 3))):
                each(has_source, lambda h, k=k: wave(k, h).wait_recv(), sides)
                got = unpacked(k, sides)
                product = dot(left_pieces(got), nn_ref[:, 0 : 4 * LANES])
                at = slice(part * wide, (part + 1) * wide)
                spread(g_halo_ref, part * wide, product)
                add(c, rows_of(then), gather(halo_m_ref[c, rows_of(then), at], g_halo_ref[at, :]))
            predict(k + 1)
            send(k + 1)
            for d in rest:
                add(c, rows_of(d), gather(halo_m_ref[c, rows_of(d), :], g_halo_ref[...]))


def shards(n_slab, n_sub, adjoint, elem_scale, cluster, face_links, halo_list, k_matrix, w_self, w_neighbour):
    dofs, elems = adjoint.shape
    per = 4 * CAP
    slots = 3 * per
    padded = 5 * LANES
    count = len(LEVELS)
    operands = (
        adjoint,
        elem_scale.reshape(1, elems),
        cluster.reshape(1, elems),
        face_links,
        halo_list,
        k_matrix,
        w_self,
        w_neighbour,
    )
    return pl.pallas_call(
        functools.partial(kernel, n_slab, n_sub),
        out_shape=jax.ShapeDtypeStruct((dofs, elems), F32),
        in_specs=[pl.BlockSpec(memory_space=pltpu.HBM)] * 8,
        out_specs=pl.BlockSpec(memory_space=pltpu.VMEM),
        scratch_shapes=[pltpu.VMEM(x.shape, x.dtype) for x in operands]
        + [
            pltpu.VMEM((2 * LANES, elems), BF16),
            pltpu.VMEM((2 * LANES, elems), BF16),
            pltpu.VMEM((elems, elems), BF16),
            pltpu.VMEM((slots, elems), BF16),
            pltpu.VMEM((padded, elems), BF16),
            pltpu.VMEM((padded, LANES), F32),
            pltpu.VMEM((slots, LANES), F32),
            pltpu.VMEM((3, slots, LANES), F32),
            pltpu.VMEM((9, slots, LANES), F32),
            pltpu.VMEM((3, slots, 4 * per), BF16),
            pltpu.VMEM((3, slots, 4 * per), BF16),
            pltpu.VMEM((4, per, elems), BF16),
            pltpu.VMEM((4 * per, 2 * LANES), BF16),
            pltpu.VMEM((4 * per, 2 * LANES), BF16),
            pltpu.VMEM((3 * LANES, 3 * LANES), BF16),
            pltpu.VMEM((3 * LANES, 5 * LANES), BF16),
            pltpu.VMEM((4 * dofs, 3 * LANES), BF16),
            pltpu.VMEM((6, LANES, LANES), F32),
            pltpu.VMEM((elems // 2, elems // 2), BF16),
            pltpu.VMEM((dofs, elems), F32),
            pltpu.VMEM((count, per, LANES), F32),
            pltpu.VMEM((count, 4 * PACKED, LANES), F32),
            pltpu.VMEM((count, 4 * PACKED, LANES), F32),
            pltpu.VMEM((3, 1, 2 * LANES), F32),
            pltpu.VMEM((3, 4, 1, 2 * LANES), F32),
            pltpu.SemaphoreType.DMA((8,)),
            pltpu.SemaphoreType.DMA((4,)),
            pltpu.SemaphoreType.DMA((2, 4)),
            pltpu.SemaphoreType.DMA((3, 4)),
            pltpu.SemaphoreType.DMA((3, 4)),
        ],
        compiler_params=pltpu.CompilerParams(
            collective_id=0, has_side_effects=True, vmem_limit_bytes=58 * 1024 * 1024
        ),
    )(*operands)


def solution(mesh):
    placed = (
        P(None, ("slab", "sub")),
        P(("slab", "sub")),
        P(("slab", "sub")),
        P(None, ("slab", "sub")),
        P(None, ("slab", "sub")),
        P(),
        P(),
        P(),
    )
    return jax.shard_map(
        functools.partial(shards, mesh.shape["slab"], mesh.shape["sub"]),
        mesh=mesh,
        in_specs=placed,
        out_specs=P(None, ("slab", "sub")),
        check_vma=False,
    )
```

```python
import functools

import jax
import jax.numpy as jnp
from jax import lax
from jax.experimental import pallas as pl
from jax.experimental.pallas import tpu as pltpu
from jax.sharding import PartitionSpec as P

MESH = pl.DeviceIdType.MESH
F32 = jnp.float32
BF16 = jnp.bfloat16

TIME_STEP = 0.125
CAP = 48
LANES = 128
PACKED = 32
SPARE = CAP - PACKED
RUN = 32
LEVELS = (2, 1, 0, 0, 1, 0, 0)


def dot(a, b):
    return lax.dot_general(a, b, (((1,), (0,)), ((), ())), preferred_element_type=F32)


def dot_nt(a, b):
    return lax.dot_general(a, b, (((1,), (1,)), ((), ())), preferred_element_type=F32)


def dot_full(a, b):
    return lax.dot_general(
        a, b, (((1,), (0,)), ((), ())), precision=lax.Precision.HIGHEST, preferred_element_type=F32
    )


def split2(x):
    hi = x.astype(BF16)
    return hi, (x - hi.astype(F32)).astype(BF16)


def left_pieces(x):
    hi, lo = split2(x)
    return jnp.concatenate([hi, lo, hi], axis=1)


def ones_where(mask):
    return jnp.where(mask, 1.0, 0.0).astype(BF16)


def kernel(
    n_slab,
    n_sub,
    adjoint_in,
    scale_in,
    cluster_in,
    links_in,
    list_in,
    k_in,
    self_in,
    neighbour_in,
    out_ref,
    adjoint_ref,
    scale_ref,
    cluster_ref,
    links_ref,
    list_ref,
    k_ref,
    self_ref,
    neighbour_ref,
    x_ref,
    moved_ref,
    h_ref,
    q_ref,
    p_ref,
    state_ref,
    factor_ref,
    powers_ref,
    linkb_ref,
    own_m_ref,
    halo_m_ref,
    last_m_ref,
    g_own_ref,
    g_halo_ref,
    kk_ref,
    nn_ref,
    ns_ref,
    pad_ref,
    before_ref,
    pre_ref,
    send_ref,
    pack_ref,
    recv_ref,
    id_send_ref,
    id_recv_ref,
    in_sem,
    send_sem,
    recv_sem,
    id_send_sem,
    id_recv_sem,
):
    dofs, elems = adjoint_ref.shape
    side = elems // 4
    per = 4 * CAP
    half = per // 2
    slots = 3 * per
    count = len(LEVELS)

    def fetch(n, src, dst):
        copy = pltpu.make_async_copy(src, dst, in_sem.at[n])
        copy.start()
        return copy

    list_copy = fetch(0, list_in, list_ref)
    cluster_copy = fetch(1, cluster_in, cluster_ref)
    k_copy = fetch(2, k_in, k_ref)
    adjoint_copy = fetch(3, adjoint_in, adjoint_ref)
    scale_copy = fetch(4, scale_in, scale_ref)
    links_copy = fetch(5, links_in, links_ref)
    neighbour_copy = fetch(6, neighbour_in, neighbour_ref)
    self_copy = fetch(7, self_in, self_ref)

    i = lax.axis_index("slab")
    j = lax.axis_index("sub")
    low = ((i - 1, j), (i, j - 1))
    has_low = (i > 0, j > 0)
    high = ((i + 1, j), (i, j + 1))
    has_high = (i < n_slab - 1, j < n_sub - 1)
    target = (low[0], high[0], low[1], high[1])
    has_target = (has_low[0], has_high[0], has_low[1], has_high[1])
    has_source = (has_high[0], has_low[0], has_high[1], has_low[1])
    link_base = (elems + side, elems, elems + 3 * side, elems + 2 * side)

    barrier = pltpu.get_barrier_semaphore()
    for h in range(4):

        @pl.when(has_target[h])
        def _(h=h):
            pl.semaphore_signal(barrier, inc=1, device_id=target[h], device_id_type=MESH)

    def wave(k, h):
        at = pl.ds(h * PACKED, PACKED)
        return pltpu.make_async_remote_copy(
            src_ref=pack_ref.at[k, at],
            dst_ref=recv_ref.at[k, at],
            send_sem=send_sem.at[h],
            recv_sem=recv_sem.at[k % 2, h],
            device_id=target[h],
            device_id_type=MESH,
        )

    def id_wave(c, h):
        return pltpu.make_async_remote_copy(
            src_ref=id_send_ref.at[c],
            dst_ref=id_recv_ref.at[c, h],
            send_sem=id_send_sem.at[c, h],
            recv_sem=id_recv_sem.at[c, h],
            device_id=target[h],
            device_id_type=MESH,
        )

    def each(has, do, sides=(2, 3, 0, 1)):
        for h in sides:

            @pl.when(has[h])
            def _(h=h):
                do(h)

    for h in range(4):

        @pl.when(jnp.logical_not(has_source[h]))
        def _(h=h):
            recv_ref[:, h * PACKED : (h + 1) * PACKED, :] = jnp.zeros((count, PACKED, LANES), F32)
            id_recv_ref[:, h] = jnp.full((3,) + id_recv_ref.shape[2:], -1.0, F32)

    before_from = lax.broadcasted_iota(jnp.int32, (2 * side, 2 * side), 0)
    before_to = lax.broadcasted_iota(jnp.int32, (2 * side, 2 * side), 1)
    before_ref[...] = ones_where(
        (before_from < before_to) & (before_from // side == before_to // side)
    )
    pad_ref[...] = jnp.zeros_like(pad_ref)
    kk_ref[...] = jnp.zeros_like(kk_ref)
    x_ref[...] = jnp.zeros_like(x_ref)
    id_send_ref[...] = jnp.full(id_send_ref.shape, -1.0, F32)
    state_ref[slots:, :] = jnp.zeros((state_ref.shape[0] - slots, LANES), F32)
    p_ref[slots:, :] = jnp.zeros((p_ref.shape[0] - slots, elems), BF16)

    list_copy.wait()
    cluster_copy.wait()
    k_copy.wait()
    adjoint_copy.wait()
    scale_copy.wait()
    links_copy.wait()

    listed = jnp.concatenate([list_ref[0:1, :], list_ref[1:2, :]], axis=1)
    h_ref[...] = ones_where(lax.broadcasted_iota(jnp.int32, (elems, elems), 0) == listed)

    aux = jnp.concatenate(
        [scale_ref[...], links_ref[...].astype(F32), jnp.zeros((11, elems), F32)], axis=0
    )
    for at, part in ((0, adjoint_ref[...]), (dofs, aux)):
        hi, lo = split2(part)
        x_ref[at : at + part.shape[0], :] = hi
        x_ref[LANES + at : LANES + at + part.shape[0], :] = lo

    cluster8 = jnp.broadcast_to(cluster_ref[...].astype(F32), (16, elems)).astype(BF16)
    by_position = dot(jnp.concatenate([cluster8, x_ref[...]], axis=0), h_ref[...])
    cluster_p = by_position[0:16, :]
    moved_ref[...] = by_position[16:, :].astype(BF16)

    level_row = lax.broadcasted_iota(jnp.int32, (16, elems), 0).astype(F32)
    is_level = cluster_p == level_row
    marks = ones_where(is_level)
    ranks = jnp.concatenate(
        [dot(marks[:, 0 : 2 * side], before_ref[...]), dot(marks[:, 2 * side :], before_ref[...])],
        axis=1,
    )
    rank = jnp.sum(jnp.where(is_level, ranks, 0.0), axis=0, keepdims=True)
    position = lax.broadcasted_iota(jnp.int32, (1, elems), 1)
    side_of = position // side
    rank = rank.astype(jnp.int32)
    within = jnp.where(
        rank < PACKED, 4 * SPARE + side_of * PACKED + rank, side_of * SPARE + rank - PACKED
    )
    slot = cluster_p[0:1, :].astype(jnp.int32) * per + within

    base = jnp.where(
        side_of == 0,
        link_base[0],
        jnp.where(side_of == 1, link_base[1], jnp.where(side_of == 2, link_base[2], link_base[3])),
    )
    own_plus = listed + 1
    far_plus = base + (position - side_of * side) + 1
    id_rows = jnp.concatenate(
        [
            (own_plus // 32 * 32).astype(F32),
            (own_plus % 32).astype(F32),
            (far_plus // 32 * 32).astype(F32),
            (far_plus % 32).astype(F32),
            jnp.zeros((12, elems), F32),
        ],
        axis=0,
    ).astype(BF16)

    def step_size(c):
        return TIME_STEP * 2.0**c

    def rows_of(c):
        return slice(c * per, (c + 1) * per)

    own_ids = {}

    def place(c):
        rows = rows_of(c)
        q = ones_where(lax.broadcasted_iota(jnp.int32, (per, elems), 0) + c * per == slot)
        ids = dot_nt(id_rows, q)
        own = ids[0:1, :] + ids[1:2, :] - 1.0
        own_ids[c] = jnp.concatenate([own, own], axis=1)
        id_send_ref[c, :, 0:per] = ids[2:3, :] + ids[3:4, :] - 1.0
        q_ref[rows, :] = q
        placed = dot_nt(q, moved_ref[...])
        placed = placed[:, 0:LANES] + placed[:, LANES:]
        lane = lax.broadcasted_iota(jnp.int32, (per, LANES), 1)
        state_ref[rows, :] = jnp.where(lane < dofs, placed, 0.0)
        factor = jnp.broadcast_to(placed[:, dofs : dofs + 1], (per, LANES))
        factor_ref[rows, :] = factor
        a = step_size(c) * factor
        powers_ref[0, rows, :] = a * (1.0 / 2.0)
        powers_ref[1, rows, :] = a * a * (1.0 / 6.0)
        powers_ref[2, rows, :] = a * a * a * (1.0 / 24.0)
        return placed

    def spread_links(c, placed):
        rows = rows_of(c)
        lane = lax.broadcasted_iota(jnp.int32, (per, LANES), 1)
        faces = [
            jnp.broadcast_to(placed[:, dofs + 1 + f : dofs + 2 + f], (per, LANES)) for f in range(4)
        ]
        linkb_ref[0, rows, :] = faces[0]
        linkb_ref[1, rows, :] = jnp.where(lane < LANES // 2, faces[0], faces[1])
        linkb_ref[2, rows, :] = faces[1]
        linkb_ref[3, rows, :] = faces[2]
        linkb_ref[4, rows, :] = jnp.where(lane < LANES // 2, faces[2], faces[3])
        linkb_ref[5, rows, :] = faces[3]
        for block in range(3):
            cut = half - block * (LANES - half)
            linkb_ref[6 + block, rows, :] = jnp.where(lane < cut, faces[block], faces[block + 1])

    def put(ref, at, matrix):
        hi, lo = split2(matrix)
        cols = slice(at * LANES, (at + 1) * LANES)
        ref[0:LANES, cols] = hi
        ref[LANES : 2 * LANES, cols] = hi
        ref[2 * LANES :, cols] = lo

    pad_ref[0, 0:dofs, 0:dofs] = k_ref[...]
    k1 = pad_ref[0].T
    k2 = dot_full(k1, k1)
    k3 = dot_full(k2, k1)
    for at, matrix in enumerate((k1, k2, k3)):
        put(kk_ref, at, matrix)

    def predict(k):
        c = LEVELS[k]
        rows = rows_of(c)
        v = state_ref[rows, :]
        terms = dot(left_pieces(v), kk_ref[...])
        w = v
        for n in range(3):
            w = w + powers_ref[n, rows, :] * terms[:, n * LANES : (n + 1) * LANES]
        send_ref[k] = w
        lane = lax.broadcasted_iota(jnp.int32, (SPARE, LANES), 1)
        for h in range(4):
            bottom = w[h * SPARE : (h + 1) * SPARE]
            for m, shift in enumerate((dofs, dofs - CAP)):
                at = h * PACKED + m * SPARE
                top = w[4 * SPARE + at : 4 * SPARE + at + SPARE]
                pack_ref[k, at : at + SPARE, :] = jnp.where(
                    lane < dofs, top, pltpu.roll(bottom, shift, 1)
                )

    def unpacked(k, part, parts=1):
        lane = lax.broadcasted_iota(jnp.int32, (SPARE, LANES), 1)
        start = part * 2 * PACKED

        def rows_at(at, size):
            return recv_ref[k, start + at : start + at + size, :]

        rows = [rows_at(0, 2 * PACKED * parts)]
        for h in range(2 * parts):
            first = rows_at(h * PACKED, SPARE)
            second = rows_at(h * PACKED + SPARE, SPARE)
            rows.append(
                jnp.where(
                    lane < LANES - dofs,
                    pltpu.roll(first, LANES - dofs, 1),
                    pltpu.roll(second, LANES - dofs + CAP, 1),
                )
            )
        return jnp.concatenate(rows, axis=0)

    def off_chip_at(h):
        return jnp.logical_and(has_target[h], even if h == 0 else jnp.logical_not(even))

    even = lax.rem(i, 2) == 0
    far = jnp.logical_or(
        jnp.logical_and(has_target[0], lax.rem(i, RUN) == 0),
        jnp.logical_and(has_target[1], lax.rem(i, RUN) == RUN - 1),
    )
    before = tuple(jnp.logical_and(off_chip_at(h), jnp.logical_or(far, h == 1)) for h in range(2))
    after = tuple(jnp.logical_and(off_chip_at(h), jnp.logical_not(jnp.logical_or(far, h == 1))) for h in range(2))
    on_chip = tuple(jnp.logical_and(has_target[h], jnp.logical_not(even) if h == 0 else even) for h in range(2))

    def send(k):
        start = lambda h: wave(k, h).start()
        each(before, start, (0, 1))
        each(has_target, start, (2, 3))
        each(after, start, (0,))
        each(on_chip, start, (0, 1))

    def build(m_ref, c, col, links_at, blocks, ids):
        for block in range(blocks):
            row = ids[:, block % 3 * LANES : (block % 3 + 1) * LANES]
            at = (col + block) * LANES
            m_ref[c, :, at : at + LANES] = ones_where(linkb_ref[links_at + block, 0:slots, :] == row)

    def spread(g_ref, at, product):
        size = product.shape[0]
        for f in range(4):
            hi, lo = split2(product[:, f * LANES : (f + 1) * LANES])
            rows = slice(at + f * size, at + (f + 1) * size)
            g_ref[rows, 0:LANES] = hi
            g_ref[rows, LANES : 2 * LANES] = lo

    def gather(m, g):
        both = dot(m, g)
        return both[:, 0:LANES] + both[:, LANES:]

    def add(c, rows, change):
        state_ref[rows, :] += step_size(c) * factor_ref[rows, :] * change

    def halo_ids(c):
        lane = lax.broadcasted_iota(jnp.int32, (1, 2 * LANES), 1)
        side_at = jnp.where(lane < 4 * SPARE, lane // SPARE, (lane - 4 * SPARE) // PACKED)
        ids = [id_recv_ref[c, h] for h in range(4)]
        return jnp.where(
            side_at == 0,
            ids[0],
            jnp.where(side_at == 1, ids[1], jnp.where(side_at == 2, ids[2], ids[3])),
        )

    first = LEVELS[0]
    placed = {first: place(first)}
    predict(0)
    pl.semaphore_wait(barrier, sum(has.astype(jnp.int32) for has in has_target))
    each(has_target, lambda h: id_wave(first, h).start())
    send(0)

    for c in (1, 0):
        placed[c] = place(c)
    each(has_target, lambda h: id_wave(1, h).start())
    each(has_target, lambda h: id_wave(0, h).start())
    for c in (2, 1, 0):
        spread_links(c, placed[c])

    neighbour_copy.wait()
    self_copy.wait()
    pad_ref[1, 0:dofs, 0:dofs] = self_ref[...]
    for f in range(4):
        pad_ref[2 + f, 0:dofs, 0:dofs] = neighbour_ref[:, f * dofs : (f + 1) * dofs]
    for f in range(4):
        put(nn_ref, f, pad_ref[2 + f].T)
        hi, lo = split2(pad_ref[2 + f, 0:dofs, :])
        ns_ref[f * dofs : (f + 1) * dofs, :] = jnp.concatenate([hi, hi, lo], axis=1)
    put(nn_ref, 4, pad_ref[1].T)

    seen = set()
    for k, c in enumerate(LEVELS):
        last = k == count - 1
        if c not in seen:
            build(own_m_ref, c, 0, 0, 6, own_ids[c])
        product = dot(left_pieces(send_ref[k]), nn_ref[...])
        spread(g_own_ref, 0, product)
        for d in range(3):
            change = gather(own_m_ref[c, rows_of(d), :], g_own_ref[...])
            if d == c:
                change = change + product[:, 4 * LANES :]
            add(c, rows_of(d), change)
        if c not in seen:
            seen.add(c)
            each(has_source, lambda h, c=c: id_wave(c, h).wait_recv())
            ids = halo_ids(c)
            for part in range(2):
                tops = 4 * SPARE + 2 * part * PACKED
                cut = [
                    ids[:, tops : tops + 2 * PACKED],
                    ids[:, 2 * part * SPARE : 2 * (part + 1) * SPARE],
                ]
                build(halo_m_ref, c, 3 * part, 6, 3, jnp.concatenate(cut * 4, axis=1))
        each(has_target, lambda h, k=k: wave(k, h).wait_send())
        if k in (1, 2, 3):
            each(has_target, lambda h, k=k: id_wave(k - 1, h).wait_send())
        if k == 3:
            p_ref[0:slots, :] = dot_nt(q_ref[...], h_ref[...]).astype(BF16)
        if last:
            ids = halo_ids(c)
            for block in range(2):
                size = min(LANES, per - block * LANES)
                at = 4 * SPARE * (1 - block)
                row = ids[:, at : at + LANES]
                column = jnp.broadcast_to(row, (LANES, LANES)).T
                column = jnp.concatenate([column] * 4, axis=1)[0:size, :]
                for f in range(4):
                    row = links_ref[f : f + 1, :].astype(F32)
                    last_m_ref[f, block * LANES : block * LANES + size, :] = ones_where(column == row)
            turned = jnp.concatenate(
                [state_ref[at * LANES : (at + 1) * LANES, :].T for at in range(5)], axis=1
            )
            both = dot(jnp.concatenate(split2(turned), axis=0), p_ref[...])
            pre_ref[...] = (both[0:LANES] + both[LANES:])[0:dofs, :]
            each(has_source, lambda h, k=k: wave(k, h).wait_recv())
            got = unpacked(k, 0, 2)
            product = dot_nt(ns_ref[...], left_pieces(got))
            total = jnp.zeros((2 * dofs, elems), F32)
            for f in range(4):
                pieces = split2(product[f * dofs : (f + 1) * dofs, :])
                total = total + dot(jnp.concatenate(pieces, axis=0), last_m_ref[f])
            a = step_size(c) * scale_ref[...]
            out_ref[...] = pre_ref[...] + a * (total[0:dofs] + total[dofs:])
        else:
            then = LEVELS[k + 1]
            rest = [d for d in range(3) if d != then]
            wide = 2 * per

            def take(parts, k=k, c=c, then=then, wide=wide):
                for part in parts:
                    each(has_source, lambda h: wave(k, h).wait_recv(), (2 * part, 2 * part + 1))
                    product = dot(left_pieces(unpacked(k, part)), nn_ref[:, 0 : 4 * LANES])
                    spread(g_halo_ref, part * wide, product)
                    at = slice(part * wide, (part + 1) * wide)
                    add(c, rows_of(then), gather(halo_m_ref[c, rows_of(then), at], g_halo_ref[at, :]))
                predict(k + 1)

            pl.when(far)(lambda: take((1, 0)))
            pl.when(jnp.logical_not(far))(lambda: take((0, 1)))
            send(k + 1)
            for d in rest:
                add(c, rows_of(d), gather(halo_m_ref[c, rows_of(d), :], g_halo_ref[...]))


def shards(n_slab, n_sub, adjoint, elem_scale, cluster, face_links, halo_list, k_matrix, w_self, w_neighbour):
    dofs, elems = adjoint.shape
    per = 4 * CAP
    slots = 3 * per
    padded = 5 * LANES
    count = len(LEVELS)
    operands = (
        adjoint,
        elem_scale.reshape(1, elems),
        cluster.reshape(1, elems),
        face_links,
        halo_list,
        k_matrix,
        w_self,
        w_neighbour,
    )
    return pl.pallas_call(
        functools.partial(kernel, n_slab, n_sub),
        out_shape=jax.ShapeDtypeStruct((dofs, elems), F32),
        in_specs=[pl.BlockSpec(memory_space=pltpu.HBM)] * 8,
        out_specs=pl.BlockSpec(memory_space=pltpu.VMEM),
        scratch_shapes=[pltpu.VMEM(x.shape, x.dtype) for x in operands]
        + [
            pltpu.VMEM((2 * LANES, elems), BF16),
            pltpu.VMEM((2 * LANES, elems), BF16),
            pltpu.VMEM((elems, elems), BF16),
            pltpu.VMEM((slots, elems), BF16),
            pltpu.VMEM((padded, elems), BF16),
            pltpu.VMEM((padded, LANES), F32),
            pltpu.VMEM((slots, LANES), F32),
            pltpu.VMEM((3, slots, LANES), F32),
            pltpu.VMEM((9, slots, LANES), F32),
            pltpu.VMEM((3, slots, 4 * per), BF16),
            pltpu.VMEM((3, slots, 4 * per), BF16),
            pltpu.VMEM((4, per, elems), BF16),
            pltpu.VMEM((4 * per, 2 * LANES), BF16),
            pltpu.VMEM((4 * per, 2 * LANES), BF16),
            pltpu.VMEM((3 * LANES, 3 * LANES), BF16),
            pltpu.VMEM((3 * LANES, 5 * LANES), BF16),
            pltpu.VMEM((4 * dofs, 3 * LANES), BF16),
            pltpu.VMEM((6, LANES, LANES), F32),
            pltpu.VMEM((elems // 2, elems // 2), BF16),
            pltpu.VMEM((dofs, elems), F32),
            pltpu.VMEM((count, per, LANES), F32),
            pltpu.VMEM((count, 4 * PACKED, LANES), F32),
            pltpu.VMEM((count, 4 * PACKED, LANES), F32),
            pltpu.VMEM((3, 1, 2 * LANES), F32),
            pltpu.VMEM((3, 4, 1, 2 * LANES), F32),
            pltpu.SemaphoreType.DMA((8,)),
            pltpu.SemaphoreType.DMA((4,)),
            pltpu.SemaphoreType.DMA((2, 4)),
            pltpu.SemaphoreType.DMA((3, 4)),
            pltpu.SemaphoreType.DMA((3, 4)),
        ],
        compiler_params=pltpu.CompilerParams(
            collective_id=0, has_side_effects=True, vmem_limit_bytes=58 * 1024 * 1024
        ),
    )(*operands)


def solution(mesh):
    placed = (
        P(None, ("slab", "sub")),
        P(("slab", "sub")),
        P(("slab", "sub")),
        P(None, ("slab", "sub")),
        P(None, ("slab", "sub")),
        P(),
        P(),
        P(),
    )
    return jax.shard_map(
        functools.partial(shards, mesh.shape["slab"], mesh.shape["sub"]),
        mesh=mesh,
        in_specs=placed,
        out_specs=P(None, ("slab", "sub")),
        check_vma=False,
    )
```

```python
import functools

import jax
import jax.numpy as jnp
from jax import lax
from jax.experimental import pallas as pl
from jax.experimental.pallas import tpu as pltpu
from jax.sharding import PartitionSpec as P

MESH = pl.DeviceIdType.MESH
F32 = jnp.float32
BF16 = jnp.bfloat16

TIME_STEP = 0.125
CAP = 48
LANES = 128
PACKED = 32
SPARE = CAP - PACKED
RUN = 32
LEVELS = (2, 1, 0, 0, 1, 0, 0)


def dot(a, b):
    return lax.dot_general(a, b, (((1,), (0,)), ((), ())), preferred_element_type=F32)


def dot_nt(a, b):
    return lax.dot_general(a, b, (((1,), (1,)), ((), ())), preferred_element_type=F32)


def dot_full(a, b):
    return lax.dot_general(
        a, b, (((1,), (0,)), ((), ())), precision=lax.Precision.HIGHEST, preferred_element_type=F32
    )


def split2(x):
    hi = x.astype(BF16)
    return hi, (x - hi.astype(F32)).astype(BF16)


def left_pieces(x):
    hi, lo = split2(x)
    return jnp.concatenate([hi, lo, hi], axis=1)


def ones_where(mask):
    return jnp.where(mask, 1.0, 0.0).astype(BF16)


def kernel(
    n_slab,
    n_sub,
    adjoint_in,
    scale_in,
    cluster_in,
    links_in,
    list_in,
    k_in,
    self_in,
    neighbour_in,
    out_ref,
    adjoint_ref,
    scale_ref,
    cluster_ref,
    links_ref,
    list_ref,
    k_ref,
    self_ref,
    neighbour_ref,
    x_ref,
    moved_ref,
    h_ref,
    q_ref,
    p_ref,
    state_ref,
    factor_ref,
    powers_ref,
    linkb_ref,
    own_m_ref,
    halo_m_ref,
    last_m_ref,
    g_own_ref,
    g_halo_ref,
    kk_ref,
    nn_ref,
    ns_ref,
    pad_ref,
    before_ref,
    pre_ref,
    send_ref,
    pack_ref,
    recv_ref,
    id_send_ref,
    id_recv_ref,
    in_sem,
    send_sem,
    recv_sem,
    id_send_sem,
    id_recv_sem,
):
    dofs, elems = adjoint_ref.shape
    side = elems // 4
    per = 4 * CAP
    half = per // 2
    slots = 3 * per
    count = len(LEVELS)

    def fetch(n, src, dst):
        copy = pltpu.make_async_copy(src, dst, in_sem.at[n])
        copy.start()
        return copy

    adjoint_copy = fetch(3, adjoint_in, adjoint_ref)
    list_copy = fetch(0, list_in, list_ref)
    cluster_copy = fetch(1, cluster_in, cluster_ref)
    k_copy = fetch(2, k_in, k_ref)
    scale_copy = fetch(4, scale_in, scale_ref)
    links_copy = fetch(5, links_in, links_ref)
    neighbour_copy = fetch(6, neighbour_in, neighbour_ref)
    self_copy = fetch(7, self_in, self_ref)

    i = lax.axis_index("slab")
    j = lax.axis_index("sub")
    low = ((i - 1, j), (i, j - 1))
    has_low = (i > 0, j > 0)
    high = ((i + 1, j), (i, j + 1))
    has_high = (i < n_slab - 1, j < n_sub - 1)
    target = (low[0], high[0], low[1], high[1])
    has_target = (has_low[0], has_high[0], has_low[1], has_high[1])
    has_source = (has_high[0], has_low[0], has_high[1], has_low[1])
    link_base = (elems + side, elems, elems + 3 * side, elems + 2 * side)

    barrier = pltpu.get_barrier_semaphore()
    for h in range(4):

        @pl.when(has_target[h])
        def _(h=h):
            pl.semaphore_signal(barrier, inc=1, device_id=target[h], device_id_type=MESH)

    def wave(k, h):
        at = pl.ds(h * PACKED, PACKED)
        return pltpu.make_async_remote_copy(
            src_ref=pack_ref.at[k, at],
            dst_ref=recv_ref.at[k, at],
            send_sem=send_sem.at[h],
            recv_sem=recv_sem.at[k % 2, h],
            device_id=target[h],
            device_id_type=MESH,
        )

    def id_wave(c, h):
        return pltpu.make_async_remote_copy(
            src_ref=id_send_ref.at[c],
            dst_ref=id_recv_ref.at[c, h],
            send_sem=id_send_sem.at[c, h],
            recv_sem=id_recv_sem.at[c, h],
            device_id=target[h],
            device_id_type=MESH,
        )

    def each(has, do, sides=(2, 3, 0, 1)):
        for h in sides:

            @pl.when(has[h])
            def _(h=h):
                do(h)

    for h in range(4):

        @pl.when(jnp.logical_not(has_source[h]))
        def _(h=h):
            recv_ref[:, h * PACKED : (h + 1) * PACKED, :] = jnp.zeros((count, PACKED, LANES), F32)
            id_recv_ref[:, h] = jnp.full((3,) + id_recv_ref.shape[2:], -1.0, F32)

    before_from = lax.broadcasted_iota(jnp.int32, (2 * side, 2 * side), 0)
    before_to = lax.broadcasted_iota(jnp.int32, (2 * side, 2 * side), 1)
    before_ref[...] = ones_where(
        (before_from < before_to) & (before_from // side == before_to // side)
    )
    pad_ref[...] = jnp.zeros_like(pad_ref)
    kk_ref[...] = jnp.zeros_like(kk_ref)
    x_ref[...] = jnp.zeros_like(x_ref)
    id_send_ref[...] = jnp.full(id_send_ref.shape, -1.0, F32)
    state_ref[slots:, :] = jnp.zeros((state_ref.shape[0] - slots, LANES), F32)
    p_ref[slots:, :] = jnp.zeros((p_ref.shape[0] - slots, elems), BF16)

    list_copy.wait()
    cluster_copy.wait()
    k_copy.wait()
    adjoint_copy.wait()
    scale_copy.wait()
    links_copy.wait()

    listed = jnp.concatenate([list_ref[0:1, :], list_ref[1:2, :]], axis=1)
    h_ref[...] = ones_where(lax.broadcasted_iota(jnp.int32, (elems, elems), 0) == listed)

    aux = jnp.concatenate(
        [scale_ref[...], links_ref[...].astype(F32), jnp.zeros((11, elems), F32)], axis=0
    )
    for at, part in ((0, adjoint_ref[...]), (dofs, aux)):
        hi, lo = split2(part)
        x_ref[at : at + part.shape[0], :] = hi
        x_ref[LANES + at : LANES + at + part.shape[0], :] = lo

    cluster8 = jnp.broadcast_to(cluster_ref[...].astype(F32), (16, elems)).astype(BF16)
    by_position = dot(jnp.concatenate([cluster8, x_ref[...]], axis=0), h_ref[...])
    cluster_p = by_position[0:16, :]
    moved_ref[...] = by_position[16:, :].astype(BF16)

    level_row = lax.broadcasted_iota(jnp.int32, (16, elems), 0).astype(F32)
    is_level = cluster_p == level_row
    marks = ones_where(is_level)
    ranks = jnp.concatenate(
        [dot(marks[:, 0 : 2 * side], before_ref[...]), dot(marks[:, 2 * side :], before_ref[...])],
        axis=1,
    )
    rank = jnp.sum(jnp.where(is_level, ranks, 0.0), axis=0, keepdims=True)
    position = lax.broadcasted_iota(jnp.int32, (1, elems), 1)
    side_of = position // side
    rank = rank.astype(jnp.int32)
    within = jnp.where(
        rank < PACKED, 4 * SPARE + side_of * PACKED + rank, side_of * SPARE + rank - PACKED
    )
    slot = cluster_p[0:1, :].astype(jnp.int32) * per + within

    base = jnp.where(
        side_of == 0,
        link_base[0],
        jnp.where(side_of == 1, link_base[1], jnp.where(side_of == 2, link_base[2], link_base[3])),
    )
    own_plus = listed + 1
    far_plus = base + (position - side_of * side) + 1
    id_rows = jnp.concatenate(
        [
            (own_plus // 32 * 32).astype(F32),
            (own_plus % 32).astype(F32),
            (far_plus // 32 * 32).astype(F32),
            (far_plus % 32).astype(F32),
            jnp.zeros((12, elems), F32),
        ],
        axis=0,
    ).astype(BF16)

    def step_size(c):
        return TIME_STEP * 2.0**c

    def rows_of(c):
        return slice(c * per, (c + 1) * per)

    own_ids = {}

    def place(c):
        rows = rows_of(c)
        q = ones_where(lax.broadcasted_iota(jnp.int32, (per, elems), 0) + c * per == slot)
        ids = dot_nt(id_rows, q)
        own = ids[0:1, :] + ids[1:2, :] - 1.0
        own_ids[c] = jnp.concatenate([own, own], axis=1)
        id_send_ref[c, :, 0:per] = ids[2:3, :] + ids[3:4, :] - 1.0
        q_ref[rows, :] = q
        placed = dot_nt(q, moved_ref[...])
        placed = placed[:, 0:LANES] + placed[:, LANES:]
        lane = lax.broadcasted_iota(jnp.int32, (per, LANES), 1)
        state_ref[rows, :] = jnp.where(lane < dofs, placed, 0.0)
        factor = jnp.broadcast_to(placed[:, dofs : dofs + 1], (per, LANES))
        factor_ref[rows, :] = factor
        a = step_size(c) * factor
        powers_ref[0, rows, :] = a * (1.0 / 2.0)
        powers_ref[1, rows, :] = a * a * (1.0 / 6.0)
        powers_ref[2, rows, :] = a * a * a * (1.0 / 24.0)
        return placed

    def spread_links(c, placed):
        rows = rows_of(c)
        lane = lax.broadcasted_iota(jnp.int32, (per, LANES), 1)
        faces = [
            jnp.broadcast_to(placed[:, dofs + 1 + f : dofs + 2 + f], (per, LANES)) for f in range(4)
        ]
        linkb_ref[0, rows, :] = faces[0]
        linkb_ref[1, rows, :] = jnp.where(lane < LANES // 2, faces[0], faces[1])
        linkb_ref[2, rows, :] = faces[1]
        linkb_ref[3, rows, :] = faces[2]
        linkb_ref[4, rows, :] = jnp.where(lane < LANES // 2, faces[2], faces[3])
        linkb_ref[5, rows, :] = faces[3]
        for block in range(3):
            cut = half - block * (LANES - half)
            linkb_ref[6 + block, rows, :] = jnp.where(lane < cut, faces[block], faces[block + 1])

    def put(ref, at, matrix):
        hi, lo = split2(matrix)
        cols = slice(at * LANES, (at + 1) * LANES)
        ref[0:LANES, cols] = hi
        ref[LANES : 2 * LANES, cols] = hi
        ref[2 * LANES :, cols] = lo

    pad_ref[0, 0:dofs, 0:dofs] = k_ref[...]
    k1 = pad_ref[0].T
    k2 = dot_full(k1, k1)
    k3 = dot_full(k2, k1)
    for at, matrix in enumerate((k1, k2, k3)):
        put(kk_ref, at, matrix)

    def predict(k):
        c = LEVELS[k]
        rows = rows_of(c)
        v = state_ref[rows, :]
        terms = dot(left_pieces(v), kk_ref[...])
        w = v
        for n in range(3):
            w = w + powers_ref[n, rows, :] * terms[:, n * LANES : (n + 1) * LANES]
        send_ref[k] = w
        lane = lax.broadcasted_iota(jnp.int32, (SPARE, LANES), 1)
        for h in range(4):
            bottom = w[h * SPARE : (h + 1) * SPARE]
            for m, shift in enumerate((dofs, dofs - CAP)):
                at = h * PACKED + m * SPARE
                top = w[4 * SPARE + at : 4 * SPARE + at + SPARE]
                pack_ref[k, at : at + SPARE, :] = jnp.where(
                    lane < dofs, top, pltpu.roll(bottom, shift, 1)
                )

    def unpacked(k, part, parts=1):
        lane = lax.broadcasted_iota(jnp.int32, (SPARE, LANES), 1)
        start = part * 2 * PACKED

        def rows_at(at, size):
            return recv_ref[k, start + at : start + at + size, :]

        rows = [rows_at(0, 2 * PACKED * parts)]
        for h in range(2 * parts):
            first = rows_at(h * PACKED, SPARE)
            second = rows_at(h * PACKED + SPARE, SPARE)
            rows.append(
                jnp.where(
                    lane < LANES - dofs,
                    pltpu.roll(first, LANES - dofs, 1),
                    pltpu.roll(second, LANES - dofs + CAP, 1),
                )
            )
        return jnp.concatenate(rows, axis=0)

    def off_chip_at(h):
        return jnp.logical_and(has_target[h], even if h == 0 else jnp.logical_not(even))

    even = lax.rem(i, 2) == 0
    far = jnp.logical_or(
        jnp.logical_and(has_target[0], lax.rem(i, RUN) == 0),
        jnp.logical_and(has_target[1], lax.rem(i, RUN) == RUN - 1),
    )
    before = tuple(jnp.logical_and(off_chip_at(h), jnp.logical_or(far, h == 1)) for h in range(2))
    after = tuple(jnp.logical_and(off_chip_at(h), jnp.logical_not(jnp.logical_or(far, h == 1))) for h in range(2))
    on_chip = tuple(jnp.logical_and(has_target[h], jnp.logical_not(even) if h == 0 else even) for h in range(2))

    def send(k):
        start = lambda h: wave(k, h).start()
        each(before, start, (0, 1))
        each(has_target, start, (2, 3))
        each(after, start, (0,))
        each(on_chip, start, (0, 1))

    def build(m_ref, c, col, links_at, blocks, ids):
        for block in range(blocks):
            row = ids[:, block % 3 * LANES : (block % 3 + 1) * LANES]
            at = (col + block) * LANES
            m_ref[c, :, at : at + LANES] = ones_where(linkb_ref[links_at + block, 0:slots, :] == row)

    def spread(g_ref, at, product):
        size = product.shape[0]
        for f in range(4):
            hi, lo = split2(product[:, f * LANES : (f + 1) * LANES])
            rows = slice(at + f * size, at + (f + 1) * size)
            g_ref[rows, 0:LANES] = hi
            g_ref[rows, LANES : 2 * LANES] = lo

    def gather(m, g):
        both = dot(m, g)
        return both[:, 0:LANES] + both[:, LANES:]

    def add(c, rows, change):
        state_ref[rows, :] += step_size(c) * factor_ref[rows, :] * change

    def halo_ids(c):
        lane = lax.broadcasted_iota(jnp.int32, (1, 2 * LANES), 1)
        side_at = jnp.where(lane < 4 * SPARE, lane // SPARE, (lane - 4 * SPARE) // PACKED)
        ids = [id_recv_ref[c, h] for h in range(4)]
        return jnp.where(
            side_at == 0,
            ids[0],
            jnp.where(side_at == 1, ids[1], jnp.where(side_at == 2, ids[2], ids[3])),
        )

    first = LEVELS[0]
    placed = {first: place(first)}
    pl.semaphore_wait(barrier, sum(has.astype(jnp.int32) for has in has_target))
    each(has_target, lambda h: id_wave(first, h).start())
    predict(0)
    send(0)

    for c in (1, 0):
        placed[c] = place(c)
    each(has_target, lambda h: id_wave(1, h).start())
    each(has_target, lambda h: id_wave(0, h).start())
    for c in (2, 1, 0):
        spread_links(c, placed[c])

    neighbour_copy.wait()
    self_copy.wait()
    pad_ref[1, 0:dofs, 0:dofs] = self_ref[...]
    for f in range(4):
        pad_ref[2 + f, 0:dofs, 0:dofs] = neighbour_ref[:, f * dofs : (f + 1) * dofs]
    for f in range(4):
        put(nn_ref, f, pad_ref[2 + f].T)
        hi, lo = split2(pad_ref[2 + f, 0:dofs, :])
        ns_ref[f * dofs : (f + 1) * dofs, :] = jnp.concatenate([hi, hi, lo], axis=1)
    put(nn_ref, 4, pad_ref[1].T)

    seen = set()
    for k, c in enumerate(LEVELS):
        last = k == count - 1
        if c not in seen:
            build(own_m_ref, c, 0, 0, 6, own_ids[c])
        product = dot(left_pieces(send_ref[k]), nn_ref[...])
        spread(g_own_ref, 0, product)
        for d in range(3):
            change = gather(own_m_ref[c, rows_of(d), :], g_own_ref[...])
            if d == c:
                change = change + product[:, 4 * LANES :]
            add(c, rows_of(d), change)
        if c not in seen:
            seen.add(c)
            each(has_source, lambda h, c=c: id_wave(c, h).wait_recv())
            ids = halo_ids(c)
            for part in range(2):
                tops = 4 * SPARE + 2 * part * PACKED
                cut = [
                    ids[:, tops : tops + 2 * PACKED],
                    ids[:, 2 * part * SPARE : 2 * (part + 1) * SPARE],
                ]
                build(halo_m_ref, c, 3 * part, 6, 3, jnp.concatenate(cut * 4, axis=1))
        each(has_target, lambda h, k=k: wave(k, h).wait_send())
        if k in (1, 2, 3):
            each(has_target, lambda h, k=k: id_wave(k - 1, h).wait_send())
        if k == 3:
            p_ref[0:slots, :] = dot_nt(q_ref[...], h_ref[...]).astype(BF16)
        if last:
            ids = halo_ids(c)
            for block in range(2):
                size = min(LANES, per - block * LANES)
                at = 4 * SPARE * (1 - block)
                row = ids[:, at : at + LANES]
                column = jnp.broadcast_to(row, (LANES, LANES)).T
                column = jnp.concatenate([column] * 4, axis=1)[0:size, :]
                for f in range(4):
                    row = links_ref[f : f + 1, :].astype(F32)
                    last_m_ref[f, block * LANES : block * LANES + size, :] = ones_where(column == row)
            turned = jnp.concatenate(
                [state_ref[at * LANES : (at + 1) * LANES, :].T for at in range(5)], axis=1
            )
            both = dot(jnp.concatenate(split2(turned), axis=0), p_ref[...])
            pre_ref[...] = (both[0:LANES] + both[LANES:])[0:dofs, :]
            each(has_source, lambda h, k=k: wave(k, h).wait_recv())
            got = unpacked(k, 0, 2)
            product = dot_nt(ns_ref[...], left_pieces(got))
            total = jnp.zeros((2 * dofs, elems), F32)
            for f in range(4):
                pieces = split2(product[f * dofs : (f + 1) * dofs, :])
                total = total + dot(jnp.concatenate(pieces, axis=0), last_m_ref[f])
            a = step_size(c) * scale_ref[...]
            out_ref[...] = pre_ref[...] + a * (total[0:dofs] + total[dofs:])
        else:
            then = LEVELS[k + 1]
            rest = [d for d in range(3) if d != then]
            wide = 2 * per

            def take(parts, k=k, c=c, then=then, wide=wide):
                for part in parts:
                    each(has_source, lambda h: wave(k, h).wait_recv(), (2 * part, 2 * part + 1))
                    product = dot(left_pieces(unpacked(k, part)), nn_ref[:, 0 : 4 * LANES])
                    spread(g_halo_ref, part * wide, product)
                    at = slice(part * wide, (part + 1) * wide)
                    add(c, rows_of(then), gather(halo_m_ref[c, rows_of(then), at], g_halo_ref[at, :]))
                predict(k + 1)

            pl.when(far)(lambda: take((1, 0)))
            pl.when(jnp.logical_not(far))(lambda: take((0, 1)))
            send(k + 1)
            for d in rest:
                add(c, rows_of(d), gather(halo_m_ref[c, rows_of(d), :], g_halo_ref[...]))


def shards(n_slab, n_sub, adjoint, elem_scale, cluster, face_links, halo_list, k_matrix, w_self, w_neighbour):
    dofs, elems = adjoint.shape
    per = 4 * CAP
    slots = 3 * per
    padded = 5 * LANES
    count = len(LEVELS)
    operands = (
        adjoint,
        elem_scale.reshape(1, elems),
        cluster.reshape(1, elems),
        face_links,
        halo_list,
        k_matrix,
        w_self,
        w_neighbour,
    )
    return pl.pallas_call(
        functools.partial(kernel, n_slab, n_sub),
        out_shape=jax.ShapeDtypeStruct((dofs, elems), F32),
        in_specs=[pl.BlockSpec(memory_space=pltpu.HBM)] * 8,
        out_specs=pl.BlockSpec(memory_space=pltpu.VMEM),
        scratch_shapes=[pltpu.VMEM(x.shape, x.dtype) for x in operands]
        + [
            pltpu.VMEM((2 * LANES, elems), BF16),
            pltpu.VMEM((2 * LANES, elems), BF16),
            pltpu.VMEM((elems, elems), BF16),
            pltpu.VMEM((slots, elems), BF16),
            pltpu.VMEM((padded, elems), BF16),
            pltpu.VMEM((padded, LANES), F32),
            pltpu.VMEM((slots, LANES), F32),
            pltpu.VMEM((3, slots, LANES), F32),
            pltpu.VMEM((9, slots, LANES), F32),
            pltpu.VMEM((3, slots, 4 * per), BF16),
            pltpu.VMEM((3, slots, 4 * per), BF16),
            pltpu.VMEM((4, per, elems), BF16),
            pltpu.VMEM((4 * per, 2 * LANES), BF16),
            pltpu.VMEM((4 * per, 2 * LANES), BF16),
            pltpu.VMEM((3 * LANES, 3 * LANES), BF16),
            pltpu.VMEM((3 * LANES, 5 * LANES), BF16),
            pltpu.VMEM((4 * dofs, 3 * LANES), BF16),
            pltpu.VMEM((6, LANES, LANES), F32),
            pltpu.VMEM((elems // 2, elems // 2), BF16),
            pltpu.VMEM((dofs, elems), F32),
            pltpu.VMEM((count, per, LANES), F32),
            pltpu.VMEM((count, 4 * PACKED, LANES), F32),
            pltpu.VMEM((count, 4 * PACKED, LANES), F32),
            pltpu.VMEM((3, 1, 2 * LANES), F32),
            pltpu.VMEM((3, 4, 1, 2 * LANES), F32),
            pltpu.SemaphoreType.DMA((8,)),
            pltpu.SemaphoreType.DMA((4,)),
            pltpu.SemaphoreType.DMA((2, 4)),
            pltpu.SemaphoreType.DMA((3, 4)),
            pltpu.SemaphoreType.DMA((3, 4)),
        ],
        compiler_params=pltpu.CompilerParams(
            collective_id=0, has_side_effects=True, vmem_limit_bytes=58 * 1024 * 1024
        ),
    )(*operands)


def solution(mesh):
    placed = (
        P(None, ("slab", "sub")),
        P(("slab", "sub")),
        P(("slab", "sub")),
        P(None, ("slab", "sub")),
        P(None, ("slab", "sub")),
        P(),
        P(),
        P(),
    )
    return jax.shard_map(
        functools.partial(shards, mesh.shape["slab"], mesh.shape["sub"]),
        mesh=mesh,
        in_specs=placed,
        out_specs=P(None, ("slab", "sub")),
        check_vma=False,
    )
```
